32 devices in a mesh: groups: 2 (over x), domain: 16 (over z, y, core).
Axes of the slice: x: 2, y: 2, z: 4, core: 2. Of those that a mesh axis runs over, the one named last changes fastest.
Arguments:
- state_low: float32 [8, 64, 4096], P('groups', None, 'domain'), parts along dimension 0, may hold values from -6 to 6
- state_high: float32 [8, 125, 4096], P('groups', None, 'domain'), parts along dimension 0, may hold values from -6 to 6
- forward_low: bfloat16 [4, 64, 4096], P('groups', None, 'domain'), parts along dimension 0, may hold values from -6 to 6
- forward_high: bfloat16 [4, 125, 4096], P('groups', None, 'domain'), parts along dimension 0, may hold values from -6 to 6
- bulk_modulus: float32 [8192], P('domain'), may hold values from 1 to 2
- buoyancy: float32 [8192], P('domain'), may hold values from 0.5 to 1
- stretch: float32 [8192], P('domain'), may hold values from 1 to 2
- live_count: int32 [2, 16], P(None, 'domain'), may hold values from 128 to 256, as said below
- face_link: int32 [6, 8192], P(None, 'domain'), may hold values from -1 to 4607, as said below
- send_faces: int32 [2, 12288], P(None, 'domain'), may hold values from 0 to 2943, as said below
- receiver_slot: int32 [2048], P('domain'), may hold values from 0 to 127
- residual: float32 [4, 2048], P('groups', 'domain'), parts along dimension 0, may hold values from -6 to 6
- model_cell: int32 [8192], P('domain'), may hold values from 0 to 8191, as said below
Outputs:
- adjoint_low: float32 [8, 64, 4096], P('groups', None, 'domain'), parts along dimension 0
- adjoint_high: float32 [8, 125, 4096], P('groups', None, 'domain'), parts along dimension 0
- gradient: float32 [16384], P(('groups', 'domain')), parts along dimension 0
The draws below stay inside these ranges and needn't reach their ends.
There are 2 independent parts, one for each index of `groups`. The reference program is written for one: setup_inputs(seed, part) draws one part's arguments, and reference() takes and returns one part's arrays. A program takes and returns all parts, laid end to end along the dimension named above; an argument that names none is the same for every part. Nothing has to cross between parts.
Inputs may be any that keep to these rules, and one draw needn't show every extreme that they name: `live_count`: some domain index has exactly 256 live slots of each order, and some has exactly 128. `face_link`: columns from 3072 on are received ones; each of them is named by exactly one face of a slot whose number within its order is below 128 on its domain index. `send_faces`: each entry is a face column f * 2 * 256 + s of a slot whose number within its order is below 128. `model_cell`: an element of domain index d maps to a cell from (d - 2) * 512 to (d + 3) * 512 - 1.
All inputs are finite; a program needn't handle non-finite values.
Results may differ from the reference program's by a relative error of at most 0.0003.
Values sent between devices are 32-bit elements; how exact they have to be, the bound alone decides.
A program may use at most 64 MiB of HBM per device.

```python
import math
import jax
import jax.numpy as jnp
import numpy as np
from jax import lax

SLOTS = 256
CELL_DEV = 512
STEPS = 2
NODES3 = 64
NODES4 = 125
FACES_SIDE = 768
ALL_SLOTS = 4096
ELEMENTS = 8192
CELLS = 8192
RECEIVERS = 2048
N_DOMAIN = 16


def live_position(slot_pick):
    half_slots = SLOTS // 2
    return slot_pick % half_slots + (slot_pick >= half_slots).astype(jnp.int32) * SLOTS


def draw_live_count(key, part):
    key = jax.random.fold_in(key, 11)
    key_one, key_two, key_three = jax.random.split(key, 3)
    counts = jax.random.randint(key_one, (2, N_DOMAIN), SLOTS // 2, SLOTS + 1)
    busiest = jax.random.randint(key_two, (2,), 0, N_DOMAIN)
    lightest = (busiest + 1 + jax.random.randint(key_three, (2,), 0, N_DOMAIN - 1)) % N_DOMAIN
    orders = jnp.arange(2)
    counts = counts.at[orders, busiest].set(SLOTS).at[orders, lightest].set(SLOTS // 2)
    return counts.astype(jnp.int32)


def draw_send_faces(key, part):
    key = jax.random.fold_in(key, 12)
    key_one, key_two = jax.random.split(key)
    shape_all = (2, FACES_SIDE * N_DOMAIN)
    face_index = jax.random.randint(key_one, shape_all, 0, 6)
    slot_pick = jax.random.randint(key_two, shape_all, 0, SLOTS)
    columns = face_index * 2 * SLOTS + live_position(slot_pick)
    columns = columns.at[0, 0].set(0).at[1, FACES_SIDE * N_DOMAIN - 1].set(11 * SLOTS + SLOTS // 2 - 1)
    return columns.astype(jnp.int32)


def link_domain(key):
    key_one, key_two, key_three = jax.random.split(key, 3)
    columns = 12 * SLOTS
    links = jax.random.randint(key_one, (columns,), 0, columns)
    boundary = jax.random.randint(key_two, (columns,), 0, 16) == 0
    links = jnp.where(boundary, -1, links)
    chosen = jax.random.permutation(key_three, 6 * SLOTS)[:2 * FACES_SIDE]
    positions = chosen // SLOTS * 2 * SLOTS + live_position(chosen % SLOTS)
    links = links.at[positions].set(columns + jnp.arange(2 * FACES_SIDE))
    return links.reshape(6, 2 * SLOTS)


def draw_face_link(key, part):
    key = jax.random.fold_in(key, 13)
    domain_keys = jax.random.split(key, N_DOMAIN)
    links = jax.vmap(link_domain)(domain_keys)
    return jnp.transpose(links, (1, 0, 2)).reshape(6, 2 * SLOTS * N_DOMAIN).astype(jnp.int32)


def draw_model_cell(key, part):
    key = jax.random.fold_in(key, 14)
    key_one, key_two = jax.random.split(key)
    total = 2 * SLOTS * N_DOMAIN
    positions = jnp.arange(total)
    domain_of = positions // (2 * SLOTS)
    within = positions % (2 * SLOTS)
    offset = jax.random.randint(key_one, (total,), -2, 3)
    offset = jnp.where(within == 0, -2, jnp.where(within == 1, 2, offset))
    target = jnp.clip(domain_of + offset, 0, N_DOMAIN - 1)
    cell_index = target * CELL_DEV + jax.random.randint(key_two, (total,), 0, CELL_DEV)
    cell_index = cell_index.at[0].set(0).at[total - 1].set(N_DOMAIN * CELL_DEV - 1)
    return cell_index.astype(jnp.int32)


def touch_ends(values, key, smallest, top_value):
    shape = values.shape
    spot = [jax.random.randint(jax.random.fold_in(key, axis), (), 0, shape[axis]) for axis in range(len(shape))]
    values = values.at[tuple(spot)].set(smallest)
    longest = shape.index(max(shape))
    spot[longest] = (spot[longest] + 1) % shape[longest]
    return values.at[tuple(spot)].set(top_value)


def steps_of(rng, shape, cuts, smallest, largest):
    def one(axis_at, blocks):
        steps = jax.random.uniform(jax.random.fold_in(jax.random.fold_in(rng, 6), axis_at), (blocks,), jnp.float32, smallest / len(cuts), largest / len(cuts))
        return jnp.repeat(jnp.exp(steps), shape[axis_at] // blocks).reshape((-1,) + (1,) * (len(shape) - axis_at - 1))

    level = one(*cuts[0])
    for cut in cuts[1:]:
        level = level * one(*cut)
    return level


def centred(rng, dims, scale, limit, cuts=(), held_as=jnp.bfloat16):
    values = jax.random.normal(rng, dims, jnp.float32) * scale
    if len(cuts) > 0:
        values = steps_of(rng, dims, cuts, -0.22, 0.18) * values
    return jnp.clip(values, min=-limit, max=limit).astype(held_as)


def setup_inputs(seed: int = 0, part: int = 0) -> dict:
    keys = jax.random.split(jax.random.key(seed), 14)
    own_keys = jax.random.split(jax.random.fold_in(keys[13], part), 14)
    state_low = centred(own_keys[0], (4, NODES3, ALL_SLOTS), 1.0, 6.0, ((2, 16),), jnp.float32)
    state_high = centred(own_keys[1], (4, NODES4, ALL_SLOTS), 1.0, 6.0, ((2, 16),), jnp.float32)
    forward_low = centred(own_keys[2], (STEPS, NODES3, ALL_SLOTS), 1.0, 6.0, ((2, 16),))
    forward_high = centred(own_keys[3], (STEPS, NODES4, ALL_SLOTS), 1.0, 6.0, ((2, 16),))
    bulk_modulus = jnp.clip(jnp.exp(math.log(2.0) - 0.6931472 * jax.random.uniform(keys[4], (ELEMENTS,), jnp.float32) ** steps_of(keys[4], (ELEMENTS,), ((0, 16),), -0.2, 0.2)), 1.0, 2.0)
    buoyancy = jnp.clip(jnp.exp(math.log(1.0) - 0.6931472 * jax.random.uniform(keys[5], (ELEMENTS,), jnp.float32) ** steps_of(keys[5], (ELEMENTS,), ((0, 16),), -0.2, 0.2)), 0.5, 1.0)
    stretch = jnp.clip(jnp.exp(math.log(2.0) - 0.6931472 * jax.random.uniform(keys[6], (ELEMENTS,), jnp.float32) ** steps_of(keys[6], (ELEMENTS,), ((0, 16),), -0.2, 0.2)), 1.0, 2.0)
    live_count = draw_live_count(jax.random.fold_in(keys[13], 71), part)
    face_link = draw_face_link(jax.random.fold_in(keys[13], 71), part)
    send_faces = draw_send_faces(jax.random.fold_in(keys[13], 71), part)
    receiver_slot = touch_ends(jax.random.randint(keys[10], (RECEIVERS,), 0, SLOTS // 2), jax.random.fold_in(keys[10], 1), 0, (SLOTS // 2) - 1).astype(jnp.int32)
    residual = centred(own_keys[11], (STEPS, RECEIVERS), 1.0, 6.0, ((1, 16),), jnp.float32)
    model_cell = draw_model_cell(jax.random.fold_in(keys[13], 71), part)
    return {"state_low": state_low, "state_high": state_high, "forward_low": forward_low, "forward_high": forward_high, "bulk_modulus": bulk_modulus, "buoyancy": buoyancy, "stretch": stretch, "live_count": live_count, "face_link": face_link, "send_faces": send_faces, "receiver_slot": receiver_slot, "residual": residual, "model_cell": model_cell}


HIGHEST = lax.Precision.HIGHEST
TIME_STEP = 0.02
SOURCE_WEIGHT = (45.0 / 32.0) ** 3

def gll_points(degree):
    if degree == 3:
        interior = math.sqrt(0.2)
        return np.array([-1.0, -interior, interior, 1.0])
    interior = math.sqrt(3.0 / 7.0)
    return np.array([-1.0, -interior, 0.0, interior, 1.0])

def gll_weights(degree):
    if degree == 3:
        return np.array([1.0 / 6.0, 5.0 / 6.0, 5.0 / 6.0, 1.0 / 6.0])
    return np.array([0.1, 49.0 / 90.0, 32.0 / 45.0, 49.0 / 90.0, 0.1])

def lagrange_table(targets, sources):
    result = np.ones((targets.shape[0], sources.shape[0]))
    for col_index in range(sources.shape[0]):
        for skip_index in range(sources.shape[0]):
            if skip_index != col_index:
                result[:, col_index] *= (targets - sources[skip_index]) / (sources[col_index] - sources[skip_index])
    return result

def derivative_table(degree):
    points = gll_points(degree)
    number = points.shape[0]
    barycentric = np.ones(number)
    for col_index in range(number):
        for skip_index in range(number):
            if skip_index != col_index:
                barycentric[col_index] /= points[col_index] - points[skip_index]
    result = np.zeros((number, number))
    for row_index in range(number):
        for col_index in range(number):
            if row_index != col_index:
                result[row_index, col_index] = barycentric[col_index] / barycentric[row_index] / (points[row_index] - points[col_index])
        result[row_index, row_index] = -np.sum(result[row_index])
    return result

def cube_weights(weights):
    return (weights[:, None, None] * weights[None, :, None] * weights[None, None, :]).reshape(-1)

def basis_tables():
    low_points = gll_points(3)
    high_points = gll_points(4)
    weight_low = cube_weights(gll_weights(3))
    weight_high = cube_weights(gll_weights(4))
    return (jnp.asarray(derivative_table(3), jnp.float32), jnp.asarray(derivative_table(4), jnp.float32), jnp.asarray(lagrange_table(high_points, low_points), jnp.float32), jnp.asarray(lagrange_table(low_points, high_points), jnp.float32), jnp.asarray(weight_low, jnp.float32), jnp.asarray(weight_high, jnp.float32))

def derive_along(matrix, field, direction):
    patterns = ('ai,ijke->ajke', 'aj,ijke->iake', 'ak,ijke->ijae')
    return jnp.einsum(patterns[direction], matrix, field, precision=HIGHEST)

def face_stack(field):
    return jnp.stack([field[0], field[-1], field[:, 0], field[:, -1], field[:, :, 0], field[:, :, -1]], axis=2)

def normal_stack(velocity):
    return jnp.stack([-velocity[0][0], velocity[0][-1], -velocity[1][:, 0], velocity[1][:, -1], -velocity[2][:, :, 0], velocity[2][:, :, -1]], axis=2)

def to_mortar(faces_low, faces_high):
    raise_map = basis_tables()[2]
    lifted = jnp.einsum('ai,bj,ijfe->abfe', raise_map, raise_map, faces_low, precision=HIGHEST)
    joined = jnp.concatenate([lifted, faces_high], axis=3)
    return joined.reshape(25, -1)

def from_mortar(jump, slot_total):
    lower_map = basis_tables()[3]
    shaped = jump.reshape(5, 5, 6, 2 * slot_total)
    jump_low = jnp.einsum('ia,jb,abfe->ijfe', lower_map, lower_map, shaped[..., :slot_total], precision=HIGHEST)
    return (jump_low, shaped[..., slot_total:])

def neighbour_traces(own_traces, remote, face_link):
    trace_table = jnp.concatenate([own_traces, remote], axis=1)
    flat_link = face_link.reshape(-1)
    picked = jnp.take(trace_table, jnp.maximum(flat_link, 0), axis=1)
    return jnp.where(flat_link >= 0, picked, 0.0)

def place_faces(direction, low_face, high_face):
    extent = low_face.shape[0]
    empty_field = jnp.zeros((extent, extent, extent, low_face.shape[-1]), jnp.float32)
    if direction == 0:
        return empty_field.at[0].add(low_face).at[extent - 1].add(high_face)
    if direction == 1:
        return empty_field.at[:, 0].add(low_face).at[:, extent - 1].add(high_face)
    return empty_field.at[:, :, 0].add(low_face).at[:, :, extent - 1].add(high_face)

def move_velocity(pressure, velocity, jump, matrix, lift_scale, buoyancy, stretch, alive_mask):
    updated = []
    for direction in range(3):
        gradient_part = derive_along(matrix, pressure, direction) + lift_scale * place_faces(direction, -jump[:, :, 2 * direction], jump[:, :, 2 * direction + 1])
        updated.append(velocity[direction] - TIME_STEP * buoyancy * stretch * gradient_part)
    return jnp.stack(updated) * alive_mask

def move_pressure(pressure, velocity, jump, matrix, lift_scale, bulk_modulus, stretch, alive_mask):
    spread = derive_along(matrix, velocity[0], 0) + derive_along(matrix, velocity[1], 1) + derive_along(matrix, velocity[2], 2)
    for direction in range(3):
        spread = spread + lift_scale * place_faces(direction, jump[:, :, 2 * direction], jump[:, :, 2 * direction + 1])
    return (pressure - TIME_STEP * bulk_modulus * stretch * spread) * alive_mask

def start_state(state_low, state_high, live_count):
    slot_total = state_low.shape[2]
    alive_low = (jnp.arange(slot_total) < live_count[0, 0]).astype(jnp.float32)
    alive_high = (jnp.arange(slot_total) < live_count[1, 0]).astype(jnp.float32)
    pressure_low = state_low[0].reshape(4, 4, 4, slot_total) * alive_low
    velocity_low = state_low[1:].reshape(3, 4, 4, 4, slot_total) * alive_low
    pressure_high = state_high[0].reshape(5, 5, 5, slot_total) * alive_high
    velocity_high = state_high[1:].reshape(3, 5, 5, 5, slot_total) * alive_high
    return (pressure_low, velocity_low, pressure_high, velocity_high, alive_low, alive_high)

def pressure_traces(pressure_low, pressure_high):
    return to_mortar(face_stack(pressure_low), face_stack(pressure_high))

def velocity_traces(velocity_low, velocity_high):
    return to_mortar(normal_stack(velocity_low), normal_stack(velocity_high))

def pick_sent(own_traces, send_faces):
    return jnp.take(own_traces, send_faces.reshape(-1), axis=1).reshape(own_traces.shape[0], 2, -1)

def velocity_half(pressure_low, velocity_low, pressure_high, velocity_high, own_traces, remote, face_link, buoyancy, stretch, alive_low, alive_high):
    derivative_low, derivative_high = basis_tables()[:2]
    slot_total = pressure_low.shape[-1]
    jump = 0.5 * (neighbour_traces(own_traces, remote, face_link) - own_traces)
    jump_low, jump_high = from_mortar(jump, slot_total)
    velocity_low = move_velocity(pressure_low, velocity_low, jump_low, derivative_low, 6.0, buoyancy[:slot_total], stretch[:slot_total], alive_low)
    velocity_high = move_velocity(pressure_high, velocity_high, jump_high, derivative_high, 10.0, buoyancy[slot_total:], stretch[slot_total:], alive_high)
    return (velocity_low, velocity_high)

def pressure_half(pressure_low, velocity_low, pressure_high, velocity_high, own_traces, remote, face_link, bulk_modulus, stretch, alive_low, alive_high, receiver_slot, residual_now, forward_low_now, forward_high_now):
    derivative_low, derivative_high, raise_map, lower_map, weight_low, weight_high = basis_tables()
    slot_total = pressure_low.shape[-1]
    jump = -0.5 * (neighbour_traces(own_traces, remote, face_link) + own_traces)
    jump_low, jump_high = from_mortar(jump, slot_total)
    stretch_low = stretch[:slot_total]
    stretch_high = stretch[slot_total:]
    modulus_high = bulk_modulus[slot_total:]
    pressure_low = move_pressure(pressure_low, velocity_low, jump_low, derivative_low, 6.0, bulk_modulus[:slot_total], stretch_low, alive_low)
    pressure_high = move_pressure(pressure_high, velocity_high, jump_high, derivative_high, 10.0, modulus_high, stretch_high, alive_high)
    source = jnp.zeros((slot_total,), jnp.float32).at[receiver_slot].add(residual_now)
    pressure_high = pressure_high.at[2, 2, 2].add(TIME_STEP * SOURCE_WEIGHT * modulus_high * stretch_high ** 3 * source)
    term_low = jnp.dot(weight_low, forward_low_now.astype(jnp.float32) * pressure_low.reshape(-1, slot_total), precision=HIGHEST) / stretch_low ** 3
    term_high = jnp.dot(weight_high, forward_high_now.astype(jnp.float32) * pressure_high.reshape(-1, slot_total), precision=HIGHEST) / stretch_high ** 3
    return (pressure_low, pressure_high, jnp.concatenate([term_low, term_high]))

def final_state(pressure, velocity):
    slot_total = pressure.shape[-1]
    return jnp.concatenate([pressure.reshape(1, -1, slot_total), velocity.reshape(3, -1, slot_total)], axis=0)

def split_domains(values):
    shaped = values.reshape(values.shape[:-1] + (N_DOMAIN, values.shape[-1] // N_DOMAIN))
    return jnp.moveaxis(shaped, -2, 0)

def join_domains(values):
    moved = jnp.moveaxis(values, 0, -2)
    return moved.reshape(moved.shape[:-2] + (moved.shape[-2] * moved.shape[-1],))

def swap_sides(outgoing):
    blank = jnp.zeros_like(outgoing[:1, :, 0])
    from_left = jnp.concatenate([blank, outgoing[:-1, :, 1]], axis=0)
    from_right = jnp.concatenate([outgoing[1:, :, 0], blank], axis=0)
    return jnp.concatenate([from_left, from_right], axis=2)

def reference(state_low, state_high, forward_low, forward_high, bulk_modulus, buoyancy, stretch, live_count, face_link, send_faces, receiver_slot, residual, model_cell):
    started = jax.vmap(start_state)(split_domains(state_low), split_domains(state_high), split_domains(live_count))
    pressure_low, velocity_low, pressure_high, velocity_high, alive_low, alive_high = started
    modulus_dev = split_domains(bulk_modulus)
    buoyancy_dev = split_domains(buoyancy)
    stretch_dev = split_domains(stretch)
    link_dev = split_domains(face_link)
    send_dev = split_domains(send_faces)
    slot_dev = split_domains(receiver_slot)
    residual_dev = split_domains(residual)
    forward_low_dev = split_domains(forward_low)
    forward_high_dev = split_domains(forward_high)
    element_terms = jnp.zeros(modulus_dev.shape, jnp.float32)
    for time_step in range(STEPS):
        own_traces = jax.vmap(pressure_traces)(pressure_low, pressure_high)
        remote = swap_sides(jax.vmap(pick_sent)(own_traces, send_dev))
        velocity_low, velocity_high = jax.vmap(velocity_half)(pressure_low, velocity_low, pressure_high, velocity_high, own_traces, remote, link_dev, buoyancy_dev, stretch_dev, alive_low, alive_high)
        own_traces = jax.vmap(velocity_traces)(velocity_low, velocity_high)
        remote = swap_sides(jax.vmap(pick_sent)(own_traces, send_dev))
        pressure_low, pressure_high, new_terms = jax.vmap(pressure_half)(pressure_low, velocity_low, pressure_high, velocity_high, own_traces, remote, link_dev, modulus_dev, stretch_dev, alive_low, alive_high, slot_dev, residual_dev[:, time_step], forward_low_dev[:, time_step], forward_high_dev[:, time_step])
        element_terms = element_terms + new_terms
    adjoint_low = join_domains(jax.vmap(final_state)(pressure_low, velocity_low))
    adjoint_high = join_domains(jax.vmap(final_state)(pressure_high, velocity_high))
    gradient = jnp.zeros((CELLS,), jnp.float32).at[model_cell].add(element_terms.reshape(-1))
    return (adjoint_low, adjoint_high, gradient)
```

```python
import functools
import math

import jax
import jax.numpy as jnp
import ml_dtypes
import numpy as np
from jax import lax
from jax.experimental import pallas as pl
from jax.experimental.pallas import tpu as pltpu
from jax.sharding import PartitionSpec as P

STEPS = 2
TIME_STEP = 0.02
SOURCE_WEIGHT = (45.0 / 32.0) ** 3
HIGHEST = lax.Precision.HIGHEST
TILE = 128
ROWS = 32
CENTRE = 62


def gll_points(degree):
    if degree == 3:
        interior = math.sqrt(0.2)
        return np.array([-1.0, -interior, interior, 1.0])
    interior = math.sqrt(3.0 / 7.0)
    return np.array([-1.0, -interior, 0.0, interior, 1.0])


def gll_weights(degree):
    if degree == 3:
        return np.array([1.0 / 6.0, 5.0 / 6.0, 5.0 / 6.0, 1.0 / 6.0])
    return np.array([0.1, 49.0 / 90.0, 32.0 / 45.0, 49.0 / 90.0, 0.1])


def lagrange_table(targets, sources):
    result = np.ones((targets.shape[0], sources.shape[0]))
    for col in range(sources.shape[0]):
        for skip in range(sources.shape[0]):
            if skip != col:
                result[:, col] *= (targets - sources[skip]) / (sources[col] - sources[skip])
    return result


def derivative_table(degree):
    points = gll_points(degree)
    number = points.shape[0]
    barycentric = np.ones(number)
    for col in range(number):
        for skip in range(number):
            if skip != col:
                barycentric[col] /= points[col] - points[skip]
    result = np.zeros((number, number))
    for row in range(number):
        for col in range(number):
            if row != col:
                result[row, col] = barycentric[col] / barycentric[row] / (points[row] - points[col])
        result[row, row] = -np.sum(result[row])
    return result


def halves(matrix):
    high = matrix.astype(ml_dtypes.bfloat16)
    low = (matrix - high.astype(np.float64)).astype(ml_dtypes.bfloat16)
    return high, low


def face_nodes(n, face):
    cube = np.arange(n**3).reshape(n, n, n)
    return np.take(cube, 0 if face % 2 == 0 else n - 1, axis=face // 2).reshape(-1)


def order_tables(degree):
    n = degree + 1
    nodes = 64 if degree == 3 else 128
    lift = 6.0 if degree == 3 else 10.0
    exact = degree == 4
    points, mortar = gll_points(degree), gll_points(4)
    up = np.eye(5) if exact else lagrange_table(mortar, points)
    down = np.eye(5) if exact else lagrange_table(points, mortar)
    up, down = np.kron(up, up), np.kron(down, down)
    trace = np.zeros((6, ROWS, nodes))
    place = np.zeros((6, nodes, ROWS))
    for face in range(6):
        at = face_nodes(n, face)
        trace[face, :25, at] = up.T
        place[face, at, :25] = down
    pressure_trace = trace.reshape(6 * ROWS, nodes)
    sign = np.array([-1.0, 1.0] * 3)
    velocity_trace = (sign[:, None, None] * trace).reshape(3, 2 * ROWS, nodes)
    diff = derivative_table(degree)
    move_v, move_p = [], []
    for a in range(3):
        parts = [np.eye(n)] * 3
        parts[a] = diff
        own = np.zeros((nodes, nodes))
        own[: n**3, : n**3] = np.kron(np.kron(parts[0], parts[1]), parts[2])
        for side in range(2):
            at = face_nodes(n, 2 * a + side)
            own[at, at] += 0.5 * lift * (1 - 2 * side)
        own_hi, own_lo = halves(own)
        for rows, first in ((move_v, -1.0), (move_p, -1.0)):
            second = 1.0 if rows is move_v else -1.0
            other = 0.5 * lift * np.concatenate([first * place[2 * a], second * place[2 * a + 1]], 1)
            hi, lo = halves(other)
            rows.append(np.concatenate([own_hi, own_hi, own_lo, hi, hi] + ([] if exact else [lo]), 1))

    def spread(matrix):
        hi, lo = halves(matrix)
        return np.concatenate([hi, hi] + ([] if exact else [lo]), -1)

    weights = gll_weights(degree)
    cube = (weights[:, None, None] * weights[None, :, None] * weights[None, None, :]).reshape(-1)
    cube = np.repeat(cube[:, None], 256, 1).astype(np.float32)
    return spread(pressure_trace), spread(velocity_trace), np.stack(move_v), np.stack(move_p), cube


def split(value):
    high = value.astype(jnp.bfloat16)
    return high, (value - high.astype(jnp.float32)).astype(jnp.bfloat16)


def times(matrix, pieces):
    return jnp.dot(matrix, jnp.concatenate(pieces, axis=0), preferred_element_type=jnp.float32)


def picked(index, sources, start):
    lane = index & (TILE - 1)
    tile = index >> 7
    parts = list(start)
    for k, ref in sources:
        here = tile == k
        for row in range(ROWS // 8):
            block = ref[8 * row : 8 * row + 8, :]
            found = jnp.take_along_axis(block, lane, axis=1, mode="promise_in_bounds")
            parts[row] = jnp.where(here, found, parts[row])
    return parts


def kernel(
    n,
    state_low, state_high, forward_low, forward_high, bulk, buoyancy, stretch, live, link, send,
    receiver, residual, cell,
    tp_low, tp_high, tv_low, tv_high, mv_low, mv_high, mp_low, mp_high, weight_low, weight_high,
    out_low, out_high, grad,
    p_low, v_low, p_high, v_high, table, outgoing, remote, nb_low, nb_high, source, terms, wanted,
    blocks, arrived, send_sem, recv_sem, gsend_sem, grecv_sem,
):
    me = lax.axis_index("domain")
    slots = state_low.shape[2]
    side_tiles = outgoing.shape[1]
    barrier = pltpu.get_barrier_semaphore()
    count = 0
    for distance in (-2, -1, 1, 2):
        there = me + distance
        exists = jnp.logical_and(there >= 0, there < n)
        count = count + exists.astype(jnp.int32)

        @pl.when(exists)
        def _():
            pl.semaphore_signal(
                barrier, inc=1, device_id={"domain": there}, device_id_type=pl.DeviceIdType.MESH
            )

    @pl.when(me == 0)
    def _():
        remote[:, 0] = jnp.zeros(remote[:, 0].shape, jnp.float32)

    @pl.when(me == n - 1)
    def _():
        remote[:, 1] = jnp.zeros(remote[:, 1].shape, jnp.float32)

    for block in (0, 1, 3, 4):
        origin = me - (block - 2)

        @pl.when(jnp.logical_or(origin < 0, origin >= n))
        def _():
            arrived[block] = jnp.zeros(arrived[block].shape, jnp.float32)

    slot = lax.broadcasted_iota(jnp.int32, (1, slots), 1)
    alive_low = (slot < live[0:1, 0:1]).astype(jnp.float32)
    alive_high = (slot < live[1:2, 0:1]).astype(jnp.float32)
    p_high[120:128, :] = jnp.zeros((8, slots), jnp.float32)
    p_low[...] = state_low[0] * alive_low
    p_high[0:125, :] = state_high[0] * alive_high
    for a in range(3):
        v_high[a, 120:128, :] = jnp.zeros((8, slots), jnp.float32)
        v_low[a] = state_low[1 + a] * alive_low
        v_high[a, 0:125, :] = state_high[1 + a] * alive_high
    stretch_low, stretch_high = stretch[:, :slots], stretch[:, slots:]
    rate_v_low = TIME_STEP * buoyancy[:, :slots] * stretch_low * alive_low
    rate_v_high = TIME_STEP * buoyancy[:, slots:] * stretch_high * alive_high
    rate_p_low = TIME_STEP * bulk[:, :slots] * stretch_low * alive_low
    rate_p_high = TIME_STEP * bulk[:, slots:] * stretch_high * alive_high
    volume_low = stretch_low * stretch_low * stretch_low
    volume_high = stretch_high * stretch_high * stretch_high
    rows = lax.broadcasted_iota(jnp.int32, (TILE, receiver.shape[1]), 0)
    at_slot = (rows == receiver[...]).astype(jnp.float32)
    shared = lax.dot_general(
        jnp.concatenate([residual[...]] * 4, axis=0), at_slot, (((1,), (1,)), ((), ())), precision=HIGHEST,
        preferred_element_type=jnp.float32,
    )
    shared = shared * (
        TIME_STEP * SOURCE_WEIGHT * bulk[:, slots : slots + TILE] * volume_high[:, :TILE]
    )
    for t in range(STEPS):
        source[t] = shared[t : t + 1]
    terms[...] = jnp.zeros(terms.shape, jnp.float32)
    for face in range(6):
        for quarter in range(4):
            wanted[face, quarter] = jnp.broadcast_to(
                link[face : face + 1, quarter * TILE : (quarter + 1) * TILE], (8, TILE)
            )

    pl.semaphore_wait(barrier, count)

    def copy_down(turn):
        return pltpu.make_async_remote_copy(
            src_ref=outgoing.at[0], dst_ref=remote.at[turn, 1],
            send_sem=send_sem.at[turn, 0], recv_sem=recv_sem.at[turn, 1],
            device_id={"domain": me - 1}, device_id_type=pl.DeviceIdType.MESH,
        )

    def copy_up(turn):
        return pltpu.make_async_remote_copy(
            src_ref=outgoing.at[1], dst_ref=remote.at[turn, 0],
            send_sem=send_sem.at[turn, 1], recv_sem=recv_sem.at[turn, 0],
            device_id={"domain": me + 1}, device_id_type=pl.DeviceIdType.MESH,
        )

    def exchange(turn, traces_low, traces_high):
        for face in range(6):
            for half in range(2):
                lanes = slice(half * TILE, (half + 1) * TILE)
                faces = slice(face * ROWS, (face + 1) * ROWS)
                table[4 * face + half] = traces_low[faces, lanes]
                table[4 * face + 2 + half] = traces_high[faces, lanes]
        lower = [(k, table.at[k]) for k in range(0, 24, 2)]
        blank = [jnp.zeros((8, TILE), jnp.float32)] * (ROWS // 8)
        for way in range(2):

            def pick_out(m, carry):
                at = pl.multiple_of(m * TILE, TILE)
                index = jnp.broadcast_to(send[way : way + 1, pl.ds(at, TILE)], (8, TILE))
                parts = picked(index, lower, blank)
                for row in range(ROWS // 8):
                    outgoing[way, m, 8 * row : 8 * row + 8, :] = parts[row]
                return carry

            lax.fori_loop(0, side_tiles, pick_out, 0)
            if way == 0:

                @pl.when(me > 0)
                def _():
                    copy_down(turn).start()
            else:

                @pl.when(me < n - 1)
                def _():
                    copy_up(turn).start()

        own = [(k, table.at[k]) for k in range(24)]

        def pick_own(face, carry):
            for quarter in range(4):
                into = nb_low if quarter < 2 else nb_high
                lanes = slice((quarter % 2) * TILE, (quarter % 2 + 1) * TILE)
                parts = picked(wanted[face, quarter], own, blank)
                for row in range(ROWS // 8):
                    into[face, 8 * row : 8 * row + 8, lanes] = parts[row]
            return carry

        lax.fori_loop(0, 6, pick_own, 0)

        @pl.when(me > 0)
        def _():
            copy_down(turn).wait_send()
            copy_up(turn).wait_recv()

        @pl.when(me < n - 1)
        def _():
            copy_up(turn).wait_send()
            copy_down(turn).wait_recv()

        far = [(24 + m, remote.at[turn, m // side_tiles, m % side_tiles]) for m in range(2 * side_tiles)]

        def pick_far(face, carry):
            for quarter in (0, 2):
                into = nb_low if quarter < 2 else nb_high
                start = [into[face, 8 * row : 8 * row + 8, :TILE] for row in range(ROWS // 8)]
                parts = picked(wanted[face, quarter], far, start)
                for row in range(ROWS // 8):
                    into[face, 8 * row : 8 * row + 8, :TILE] = parts[row]
            return carry

        lax.fori_loop(0, 6, pick_far, 0)

    def neighbours(a):
        low_hi, low_lo = split(nb_low[2 * a : 2 * a + 2].reshape(2 * ROWS, slots))
        high_hi, high_lo = split(nb_high[2 * a : 2 * a + 2].reshape(2 * ROWS, slots))
        return [low_hi, low_lo, low_hi], [high_hi, high_lo]

    def step(t, carry):
        low_hi, low_lo = split(p_low[...])
        high_hi, high_lo = split(p_high[...])
        exchange(
            2 * t,
            times(tp_low[...], [low_hi, low_lo, low_hi]),
            times(tp_high[...], [high_hi, high_lo]),
        )
        traces_low, traces_high = [], []
        for a in range(3):
            from_low, from_high = neighbours(a)
            pl_hi, pl_lo = split(p_low[...])
            ph_hi, ph_lo = split(p_high[...])
            new_low = v_low[a] - rate_v_low * times(mv_low[a], [pl_hi, pl_lo, pl_hi] + from_low)
            new_high = v_high[a] - rate_v_high * times(mv_high[a], [ph_hi, ph_lo, ph_hi] + from_high)
            v_low[a] = new_low
            v_high[a] = new_high
            low_hi, low_lo = split(new_low)
            high_hi, high_lo = split(new_high)
            traces_low.append(times(tv_low[a], [low_hi, low_lo, low_hi]))
            traces_high.append(times(tv_high[a], [high_hi, high_lo]))
        exchange(2 * t + 1, jnp.concatenate(traces_low, 0), jnp.concatenate(traces_high, 0))
        total_low, total_high = 0.0, 0.0
        for a in range(3):
            from_low, from_high = neighbours(a)
            low_hi, low_lo = split(v_low[a])
            high_hi, high_lo = split(v_high[a])
            total_low = total_low + times(mp_low[a], [low_hi, low_lo, low_hi] + from_low)
            total_high = total_high + times(mp_high[a], [high_hi, high_lo, high_hi] + from_high)
        p_low[...] = p_low[...] - rate_p_low * total_low
        p_high[...] = p_high[...] - rate_p_high * total_high
        p_high[CENTRE : CENTRE + 1, :TILE] = (
            p_high[CENTRE : CENTRE + 1, :TILE] + source[t]
        )
        weighted_low = weight_low[...] * forward_low[t].astype(jnp.float32) * p_low[...]
        weighted_high = weight_high[...] * forward_high[t].astype(jnp.float32) * p_high[0:125, :]
        terms[:, :slots] += jnp.sum(weighted_low, axis=0, keepdims=True) / volume_low
        terms[:, slots:] += jnp.sum(weighted_high, axis=0, keepdims=True) / volume_high
        return carry

    lax.fori_loop(0, STEPS, step, 0)

    cells = 2 * slots
    relative = cell[...] - (me - 2) * cells
    group = relative >> 7
    group = (group >> 2) * 8 + (group & 3)
    spread_terms = jnp.where(
        lax.broadcasted_iota(jnp.int32, (40, cells), 0) == group, terms[...], 0.0
    )
    lane = (lax.broadcasted_iota(jnp.int32, (TILE, cells), 0) == (relative & (TILE - 1))).astype(
        jnp.float32
    )
    window = lax.dot_general(
        spread_terms, lane, (((1,), (1,)), ((), ())), precision=HIGHEST,
        preferred_element_type=jnp.float32,
    )
    blocks[...] = window.reshape(5, 8, TILE)

    def gradient_copy(block):
        return pltpu.make_async_remote_copy(
            src_ref=blocks.at[block], dst_ref=arrived.at[block],
            send_sem=gsend_sem.at[block], recv_sem=grecv_sem.at[block],
            device_id={"domain": me + (block - 2)}, device_id_type=pl.DeviceIdType.MESH,
        )

    for block in (0, 4, 1, 3):
        there = me + (block - 2)

        @pl.when(jnp.logical_and(there >= 0, there < n))
        def _():
            gradient_copy(block).start()

    out_low[0] = p_low[...]
    out_high[0] = p_high[0:125, :]
    for a in range(3):
        out_low[1 + a] = v_low[a]
        out_high[1 + a] = v_high[a, 0:125, :]
    for block in (0, 4, 1, 3):
        there = me + (block - 2)
        origin = me - (block - 2)

        @pl.when(jnp.logical_and(there >= 0, there < n))
        def _():
            gradient_copy(block).wait_send()

        @pl.when(jnp.logical_and(origin >= 0, origin < n))
        def _():
            gradient_copy(block).wait_recv()

    total = blocks[2]
    for block in (0, 1, 3, 4):
        total = total + arrived[block]
    grad[...] = total[:4]


def shards(n, state_low, state_high, forward_low, forward_high, bulk_modulus, buoyancy, stretch,
           live_count, face_link, send_faces, receiver_slot, residual, model_cell):
    tp_low, tv_low, mv_low, mp_low, weight_low = order_tables(3)
    tp_high, tv_high, mv_high, mp_high, weight_high = order_tables(4)
    tables = [tp_low, tp_high, tv_low, tv_high, mv_low, mv_high, mp_low, mp_high, weight_low, weight_high]
    slots = state_low.shape[2]
    side_tiles = send_faces.shape[1] // TILE
    vmem = pl.BlockSpec(memory_space=pltpu.VMEM)
    out_low, out_high, grad = pl.pallas_call(
        functools.partial(kernel, n),
        out_shape=(
            jax.ShapeDtypeStruct(state_low.shape, jnp.float32),
            jax.ShapeDtypeStruct(state_high.shape, jnp.float32),
            jax.ShapeDtypeStruct((2 * slots // TILE, TILE), jnp.float32),
        ),
        in_specs=[vmem] * (13 + len(tables)),
        out_specs=(vmem, vmem, vmem),
        scratch_shapes=[
            pltpu.VMEM((64, slots), jnp.float32),
            pltpu.VMEM((3, 64, slots), jnp.float32),
            pltpu.VMEM((128, slots), jnp.float32),
            pltpu.VMEM((3, 128, slots), jnp.float32),
            pltpu.VMEM((24, ROWS, TILE), jnp.float32),
            pltpu.VMEM((2, side_tiles, ROWS, TILE), jnp.float32),
            pltpu.VMEM((2 * STEPS, 2, side_tiles, ROWS, TILE), jnp.float32),
            pltpu.VMEM((6, ROWS, slots), jnp.float32),
            pltpu.VMEM((6, ROWS, slots), jnp.float32),
            pltpu.VMEM((STEPS, 1, TILE), jnp.float32),
            pltpu.VMEM((1, 2 * slots), jnp.float32),
            pltpu.VMEM((6, 4, 8, TILE), jnp.int32),
            pltpu.VMEM((5, 8, TILE), jnp.float32),
            pltpu.VMEM((5, 8, TILE), jnp.float32),
            pltpu.SemaphoreType.DMA((2 * STEPS, 2)),
            pltpu.SemaphoreType.DMA((2 * STEPS, 2)),
            pltpu.SemaphoreType.DMA((5,)),
            pltpu.SemaphoreType.DMA((5,)),
        ],
        compiler_params=pltpu.CompilerParams(
            collective_id=0, has_side_effects=True, vmem_limit_bytes=32 * 1024 * 1024
        ),
    )(
        state_low, state_high, forward_low, forward_high, bulk_modulus.reshape(1, -1),
        buoyancy.reshape(1, -1), stretch.reshape(1, -1), live_count, face_link, send_faces,
        receiver_slot.reshape(1, -1), residual, model_cell.reshape(1, -1),
        *[jnp.asarray(table) for table in tables],
    )
    return out_low, out_high, grad.reshape(-1)


def solution(mesh):
    placed = (
        P("groups", None, "domain"),
        P("groups", None, "domain"),
        P("groups", None, "domain"),
        P("groups", None, "domain"),
        P("domain"),
        P("domain"),
        P("domain"),
        P(None, "domain"),
        P(None, "domain"),
        P(None, "domain"),
        P("domain"),
        P("groups", "domain"),
        P("domain"),
    )
    return jax.shard_map(
        functools.partial(shards, mesh.shape["domain"]),
        mesh=mesh,
        in_specs=placed,
        out_specs=(
            P("groups", None, "domain"),
            P("groups", None, "domain"),
            P(("groups", "domain")),
        ),
        check_vma=False,
    )
```

```python
import functools
import math

import jax
import jax.numpy as jnp
import ml_dtypes
import numpy as np
from jax import lax
from jax.experimental import pallas as pl
from jax.experimental.pallas import tpu as pltpu
from jax.sharding import PartitionSpec as P

STEPS = 2
TIME_STEP = 0.02
SOURCE_WEIGHT = (45.0 / 32.0) ** 3
HIGHEST = lax.Precision.HIGHEST
TILE = 128
ROWS = 24
FACE_ROWS = 6 * ROWS + 8
LOAD_ORDER = tuple(range(21))
VMEM_GRANT = 63 * 1024 * 1024
CENTRE = 62


def gll_points(degree):
    if degree == 3:
        interior = math.sqrt(0.2)
        return np.array([-1.0, -interior, interior, 1.0])
    interior = math.sqrt(3.0 / 7.0)
    return np.array([-1.0, -interior, 0.0, interior, 1.0])


def gll_weights(degree):
    if degree == 3:
        return np.array([1.0 / 6.0, 5.0 / 6.0, 5.0 / 6.0, 1.0 / 6.0])
    return np.array([0.1, 49.0 / 90.0, 32.0 / 45.0, 49.0 / 90.0, 0.1])


def lagrange_table(targets, sources):
    result = np.ones((targets.shape[0], sources.shape[0]))
    for col in range(sources.shape[0]):
        for skip in range(sources.shape[0]):
            if skip != col:
                result[:, col] *= (targets - sources[skip]) / (sources[col] - sources[skip])
    return result


def derivative_table(degree):
    points = gll_points(degree)
    number = points.shape[0]
    barycentric = np.ones(number)
    for col in range(number):
        for skip in range(number):
            if skip != col:
                barycentric[col] /= points[col] - points[skip]
    result = np.zeros((number, number))
    for row in range(number):
        for col in range(number):
            if row != col:
                result[row, col] = barycentric[col] / barycentric[row] / (points[row] - points[col])
        result[row, row] = -np.sum(result[row])
    return result


def halves(matrix):
    high = matrix.astype(ml_dtypes.bfloat16)
    low = (matrix - high.astype(np.float64)).astype(ml_dtypes.bfloat16)
    return high, low


def face_nodes(n, face):
    cube = np.arange(n**3).reshape(n, n, n)
    return np.take(cube, 0 if face % 2 == 0 else n - 1, axis=face // 2).reshape(-1)


def order_tables(degree):
    n = degree + 1
    nodes = 64 if degree == 3 else 128
    lift = 6.0 if degree == 3 else 10.0
    exact = degree == 4
    points, mortar = gll_points(degree), gll_points(4)
    up = np.eye(5) if exact else lagrange_table(mortar, points)
    down = np.eye(5) if exact else lagrange_table(points, mortar)
    up, down = np.kron(up, up), np.kron(down, down)
    sign = np.array([-1.0, 1.0] * 3)
    pressure_trace = np.zeros((FACE_ROWS, nodes))
    velocity_trace = np.zeros((3, FACE_ROWS, nodes))
    place = np.zeros((6, nodes, 25))
    for face in range(6):
        at = face_nodes(n, face)
        rows = np.append(face * ROWS + np.arange(ROWS), 6 * ROWS + face)
        pressure_trace[np.ix_(rows, at)] = up
        velocity_trace[face // 2][np.ix_(rows, at)] = sign[face] * up
        place[face, at] = down
    velocity_trace = np.concatenate(
        [
            np.concatenate([velocity_trace[a, 2 * a * ROWS : 2 * (a + 1) * ROWS], velocity_trace[a, 6 * ROWS :]])
            for a in range(3)
        ]
    ).reshape(3, 2 * ROWS + 8, nodes)
    diff = derivative_table(degree)
    move_v, move_p = [], []
    for a in range(3):
        parts = [np.eye(n)] * 3
        parts[a] = diff
        own = np.zeros((nodes, nodes))
        own[: n**3, : n**3] = np.kron(np.kron(parts[0], parts[1]), parts[2])
        for side in range(2):
            at = face_nodes(n, 2 * a + side)
            own[at, at] += 0.5 * lift * (1 - 2 * side)
        own_hi, own_lo = halves(own)
        for rows, first in ((move_v, -1.0), (move_p, -1.0)):
            second = 1.0 if rows is move_v else -1.0
            other = np.zeros((nodes, 64))
            for side, factor in enumerate((first, second)):
                column = side * ROWS
                other[:, column : column + ROWS] = 0.5 * lift * factor * place[2 * a + side][:, :ROWS]
                other[:, 2 * ROWS + 2 * a + side] = 0.5 * lift * factor * place[2 * a + side][:, ROWS]
            hi, lo = halves(other)
            rows.append(np.concatenate([own_hi, own_hi, own_lo, hi, hi] + ([] if exact else [lo]), 1))

    def spread(matrix):
        hi, lo = halves(matrix)
        return np.concatenate([hi, hi] + ([] if exact else [lo]), -1)

    weights = gll_weights(degree)
    cube = (weights[:, None, None] * weights[None, :, None] * weights[None, None, :]).reshape(-1)
    cube = np.repeat(cube[:, None], 256, 1).astype(np.float32)
    return spread(pressure_trace), spread(velocity_trace), np.stack(move_v), np.stack(move_p), cube


def split(value):
    high = value.astype(jnp.bfloat16)
    return high, (value - high.astype(jnp.float32)).astype(jnp.bfloat16)


def times(matrix, pieces):
    return jnp.dot(matrix, jnp.concatenate(pieces, axis=0), preferred_element_type=jnp.float32)


def picked(index, sources, lasts, start, last):
    lane = index & (TILE - 1)
    tile = index >> 7
    parts = list(start)
    for k, load in sources:
        here = tile == k
        for row in range(ROWS // 8):
            found = jnp.take_along_axis(load(row), lane, axis=1, mode="promise_in_bounds")
            parts[row] = jnp.where(here, found, parts[row])
    sublane = lax.broadcasted_iota(jnp.int32, (8, TILE), 0)
    for first, stride, load in lasts:
        found = jnp.take_along_axis(load(), lane, axis=1, mode="promise_in_bounds")
        last = jnp.where(tile == first + stride * sublane, found, last)
    return parts, last


def kernel(
    n, live, *refs
):
    count = 21
    hbm, outs, vmem = refs[:count], refs[count : count + 3], refs[count + 3 : 2 * count + 3]
    body(n, live, hbm, *vmem, *outs, *refs[2 * count + 3 :])


def body(
    n, live, hbm,
    state_low, state_high, forward_low, forward_high, bulk, buoyancy, stretch, link, send,
    receiver, residual, cell,
    tables_low, tables_high, tv_low, tv_high, mv_low, mv_high, mp_low, mp_high, weights,
    out_low, out_high, grad,
    p_low, v_low, p_high, v_high, table, outgoing, remote, near, near_last, source, terms, wanted,
    blocks, arrived, send_sem, recv_sem, gsend_sem, grecv_sem, load_sem,
):
    me = lax.axis_index("domain")
    held = (
        state_low, state_high, forward_low, forward_high, bulk, buoyancy, stretch, link, send,
        receiver, residual, cell,
        tables_low, tables_high, tv_low, tv_high, mv_low, mv_high, mp_low, mp_high, weights,
    )
    loads = [
        pltpu.make_async_copy(source_ref, target, load_sem.at[i])
        for i, (source_ref, target) in enumerate(zip(hbm, held))
    ]
    for i in LOAD_ORDER:
        loads[i].start()
    slots = state_low.shape[2]
    side_tiles = send.shape[1] // TILE
    barrier = pltpu.get_barrier_semaphore()
    count = 0
    for distance in (-2, -1, 1, 2):
        there = me + distance
        exists = jnp.logical_and(there >= 0, there < n)
        count = count + exists.astype(jnp.int32)

        @pl.when(exists)
        def _():
            pl.semaphore_signal(
                barrier, inc=1, device_id={"domain": there}, device_id_type=pl.DeviceIdType.MESH
            )

    @pl.when(me == 0)
    def _():
        remote[:, 0] = jnp.zeros(remote[:, 0].shape, jnp.float32)

    @pl.when(me == n - 1)
    def _():
        remote[:, 1] = jnp.zeros(remote[:, 1].shape, jnp.float32)

    for block in (0, 1, 3, 4):
        origin = me - (block - 2)

        @pl.when(jnp.logical_or(origin < 0, origin >= n))
        def _():
            arrived[block] = jnp.zeros(arrived[block].shape, jnp.float32)

    for load in loads:
        load.wait()
    slot = lax.broadcasted_iota(jnp.int32, (1, slots), 1)
    alive_low = (slot < live[0, 0]).astype(jnp.float32)
    alive_high = (slot < live[0, 1]).astype(jnp.float32)
    p_high[120:128, :] = jnp.zeros((8, slots), jnp.float32)
    p_low[...] = state_low[0] * alive_low
    p_high[0:125, :] = state_high[0] * alive_high
    for a in range(3):
        v_high[a, 120:128, :] = jnp.zeros((8, slots), jnp.float32)
        v_low[a] = state_low[1 + a] * alive_low
        v_high[a, 0:125, :] = state_high[1 + a] * alive_high
    stretch_low, stretch_high = stretch[:, :slots], stretch[:, slots:]
    rate_v_low = TIME_STEP * buoyancy[:, :slots] * stretch_low * alive_low
    rate_v_high = TIME_STEP * buoyancy[:, slots:] * stretch_high * alive_high
    rate_p_low = TIME_STEP * bulk[:, :slots] * stretch_low * alive_low
    rate_p_high = TIME_STEP * bulk[:, slots:] * stretch_high * alive_high
    volume_low = stretch_low * stretch_low * stretch_low
    volume_high = stretch_high * stretch_high * stretch_high
    rows = lax.broadcasted_iota(jnp.int32, (TILE, receiver.shape[1]), 0)
    at_slot = (rows == receiver[...]).astype(jnp.float32)
    shared = lax.dot_general(
        jnp.concatenate([residual[...]] * 4, axis=0), at_slot, (((1,), (1,)), ((), ())), precision=HIGHEST,
        preferred_element_type=jnp.float32,
    )
    shared = shared * (
        TIME_STEP * SOURCE_WEIGHT * bulk[:, slots : slots + TILE] * volume_high[:, :TILE]
    )
    for t in range(STEPS):
        source[t] = shared[t : t + 1]
    terms[...] = jnp.zeros(terms.shape, jnp.float32)
    for face in range(6):
        for quarter in range(4):
            wanted[face, quarter] = jnp.broadcast_to(
                link[face : face + 1, quarter * TILE : (quarter + 1) * TILE], (8, TILE)
            )

    pl.semaphore_wait(barrier, count)

    def copy_down(turn):
        return pltpu.make_async_remote_copy(
            src_ref=outgoing.at[0], dst_ref=remote.at[turn, 1],
            send_sem=send_sem.at[turn, 0], recv_sem=recv_sem.at[turn, 1],
            device_id={"domain": me - 1}, device_id_type=pl.DeviceIdType.MESH,
        )

    def copy_up(turn):
        return pltpu.make_async_remote_copy(
            src_ref=outgoing.at[1], dst_ref=remote.at[turn, 0],
            send_sem=send_sem.at[turn, 1], recv_sem=recv_sem.at[turn, 0],
            device_id={"domain": me + 1}, device_id_type=pl.DeviceIdType.MESH,
        )

    def exchange(turn, traces_low, traces_high):
        for quarter, traces in enumerate((traces_low, traces_low, traces_high, traces_high)):
            table[quarter] = traces[:, (quarter % 2) * TILE : (quarter % 2 + 1) * TILE]

        def load_own(k):
            return lambda row: table[k % 4, (k // 4) * ROWS + 8 * row : (k // 4) * ROWS + 8 * row + 8, :]

        def load_own_last(quarter):
            return lambda: table[quarter, 6 * ROWS :, :]

        lower = [(k, load_own(k)) for k in range(0, 24, 2)]
        lower_last = [(quarter, 4, load_own_last(quarter)) for quarter in (0, 2)]
        zero = jnp.zeros((8, TILE), jnp.float32)
        blank = [zero] * (ROWS // 8)
        sublane = lax.broadcasted_iota(jnp.int32, (8, TILE), 0)
        for way in range(2):

            def pick_out(m, lasts):
                at = pl.multiple_of(m * TILE, TILE)
                index = jnp.broadcast_to(send[way : way + 1, pl.ds(at, TILE)], (8, TILE))
                parts, last = picked(index, lower, lower_last, blank, zero)
                for row in range(ROWS // 8):
                    into = pl.multiple_of(m * ROWS + 8 * row, 8)
                    outgoing[way, pl.ds(into, 8), :] = parts[row]
                return jnp.where(sublane == m, jnp.sum(last, axis=0, keepdims=True), lasts)

            outgoing[way, side_tiles * ROWS :, :] = lax.fori_loop(0, side_tiles, pick_out, zero)
            if way == 0:

                @pl.when(me > 0)
                def _():
                    copy_down(turn).start()
            else:

                @pl.when(me < n - 1)
                def _():
                    copy_up(turn).start()

        own = [(k, load_own(k)) for k in range(24)]
        own_last = [(quarter, 4, load_own_last(quarter)) for quarter in range(4)]

        def pick_own(face, lasts):
            result = []
            for quarter in range(4):
                parts, last = picked(wanted[face, quarter], own, own_last, blank, zero)
                for row in range(ROWS // 8):
                    near[quarter, face, 8 * row : 8 * row + 8, :] = parts[row]
                result.append(
                    jnp.where(sublane == face, jnp.sum(last, axis=0, keepdims=True), lasts[quarter])
                )
            return tuple(result)

        lasts = lax.fori_loop(0, 6, pick_own, (zero,) * 4)
        for quarter in range(4):
            near_last[quarter] = lasts[quarter]

        @pl.when(me > 0)
        def _():
            copy_down(turn).wait_send()
            copy_up(turn).wait_recv()

        @pl.when(me < n - 1)
        def _():
            copy_up(turn).wait_send()
            copy_down(turn).wait_recv()

        def load_far(m):
            way, first = m // side_tiles, (m % side_tiles) * ROWS
            return lambda row: remote[turn, way, first + 8 * row : first + 8 * row + 8, :]

        def load_far_last(way):
            return lambda: remote[turn, way, side_tiles * ROWS :, :]

        far = [(24 + m, load_far(m)) for m in range(2 * side_tiles)]
        far_last = [(24 + way * side_tiles, 1, load_far_last(way)) for way in range(2)]

        def pick_far(face, lasts):
            result = []
            for place, quarter in enumerate((0, 2)):
                start = [near[quarter, face, 8 * row : 8 * row + 8, :] for row in range(ROWS // 8)]
                parts, last = picked(wanted[face, quarter], far, far_last, start, zero)
                for row in range(ROWS // 8):
                    near[quarter, face, 8 * row : 8 * row + 8, :] = parts[row]
                result.append(
                    jnp.where(sublane == face, jnp.sum(last, axis=0, keepdims=True), lasts[place])
                )
            return tuple(result)

        lasts = lax.fori_loop(0, 6, pick_far, (zero,) * 2)
        near_last[0] += lasts[0]
        near_last[2] += lasts[1]

    def neighbours(a):
        pieces = []
        for order in range(2):
            sides = []
            for half in range(2):
                quarter = 2 * order + half
                sides.append(
                    jnp.concatenate(
                        [
                            near[quarter, 2 * a],
                            near[quarter, 2 * a + 1],
                            near_last[quarter],
                            jnp.zeros((8, TILE), jnp.float32),
                        ],
                        axis=0,
                    )
                )
            pieces.append(split(jnp.concatenate(sides, axis=1)))
        (low_hi, low_lo), (high_hi, high_lo) = pieces
        return [low_hi, low_lo, low_hi], [high_hi, high_lo]

    def joined(traces):
        faces = [trace[: 2 * ROWS] for trace in traces]
        return jnp.concatenate(faces + [sum(trace[2 * ROWS :] for trace in traces)], axis=0)

    def step(t, carry):
        low_hi, low_lo = split(p_low[...])
        high_hi, high_lo = split(p_high[...])
        exchange(
            2 * t,
            times(tables_low[...], [low_hi, low_lo, low_hi]),
            times(tables_high[...], [high_hi, high_lo]),
        )
        traces_low, traces_high = [], []
        for a in range(3):
            from_low, from_high = neighbours(a)
            pl_hi, pl_lo = split(p_low[...])
            ph_hi, ph_lo = split(p_high[...])
            new_low = v_low[a] - rate_v_low * times(mv_low[a], [pl_hi, pl_lo, pl_hi] + from_low)
            new_high = v_high[a] - rate_v_high * times(mv_high[a], [ph_hi, ph_lo, ph_hi] + from_high)
            v_low[a] = new_low
            v_high[a] = new_high
            low_hi, low_lo = split(new_low)
            high_hi, high_lo = split(new_high)
            traces_low.append(times(tv_low[a], [low_hi, low_lo, low_hi]))
            traces_high.append(times(tv_high[a], [high_hi, high_lo]))
        exchange(2 * t + 1, joined(traces_low), joined(traces_high))
        total_low, total_high = 0.0, 0.0
        for a in range(3):
            from_low, from_high = neighbours(a)
            low_hi, low_lo = split(v_low[a])
            high_hi, high_lo = split(v_high[a])
            total_low = total_low + times(mp_low[a], [low_hi, low_lo, low_hi] + from_low)
            total_high = total_high + times(mp_high[a], [high_hi, high_lo, high_hi] + from_high)
        p_low[...] = p_low[...] - rate_p_low * total_low
        p_high[...] = p_high[...] - rate_p_high * total_high
        p_high[CENTRE : CENTRE + 1, :TILE] = (
            p_high[CENTRE : CENTRE + 1, :TILE] + source[t]
        )
        weighted_low = weights[0:64] * forward_low[t].astype(jnp.float32) * p_low[...]
        weighted_high = weights[64:189] * forward_high[t].astype(jnp.float32) * p_high[0:125, :]
        terms[:, :slots] += jnp.sum(weighted_low, axis=0, keepdims=True) / volume_low
        terms[:, slots:] += jnp.sum(weighted_high, axis=0, keepdims=True) / volume_high
        return carry

    lax.fori_loop(0, STEPS, step, 0)

    cells = 2 * slots
    relative = cell[...] - (me - 2) * cells
    group = relative >> 7
    group = (group >> 2) * 8 + (group & 3)
    spread_terms = jnp.where(
        lax.broadcasted_iota(jnp.int32, (40, cells), 0) == group, terms[...], 0.0
    )
    lane = (lax.broadcasted_iota(jnp.int32, (TILE, cells), 0) == (relative & (TILE - 1))).astype(
        jnp.float32
    )
    window = lax.dot_general(
        spread_terms, lane, (((1,), (1,)), ((), ())), precision=HIGHEST,
        preferred_element_type=jnp.float32,
    )
    blocks[...] = window.reshape(5, 8, TILE)

    def gradient_copy(block):
        return pltpu.make_async_remote_copy(
            src_ref=blocks.at[block], dst_ref=arrived.at[block],
            send_sem=gsend_sem.at[block], recv_sem=grecv_sem.at[block],
            device_id={"domain": me + (block - 2)}, device_id_type=pl.DeviceIdType.MESH,
        )

    for block in (0, 4, 1, 3):
        there = me + (block - 2)

        @pl.when(jnp.logical_and(there >= 0, there < n))
        def _():
            gradient_copy(block).start()

    out_low[0] = p_low[...]
    out_high[0] = p_high[0:125, :]
    for a in range(3):
        out_low[1 + a] = v_low[a]
        out_high[1 + a] = v_high[a, 0:125, :]
    for block in (0, 4, 1, 3):
        there = me + (block - 2)
        origin = me - (block - 2)

        @pl.when(jnp.logical_and(there >= 0, there < n))
        def _():
            gradient_copy(block).wait_send()

        @pl.when(jnp.logical_and(origin >= 0, origin < n))
        def _():
            gradient_copy(block).wait_recv()

    total = blocks[2]
    for block in (0, 1, 3, 4):
        total = total + arrived[block]
    grad[...] = total[:4]


def shards(n, state_low, state_high, forward_low, forward_high, bulk_modulus, buoyancy, stretch,
           live_count, face_link, send_faces, receiver_slot, residual, model_cell):
    tp_low, tv_low, mv_low, mp_low, weight_low = order_tables(3)
    tp_high, tv_high, mv_high, mp_high, weight_high = order_tables(4)
    tables = [tp_low, tp_high, tv_low, tv_high, mv_low, mv_high, mp_low, mp_high, np.concatenate([weight_low, weight_high])]
    slots = state_low.shape[2]
    side_tiles = send_faces.shape[1] // TILE
    vmem = pl.BlockSpec(memory_space=pltpu.VMEM)
    operands = [
        state_low, state_high, forward_low, forward_high, bulk_modulus.reshape(1, -1),
        buoyancy.reshape(1, -1), stretch.reshape(1, -1), face_link, send_faces,
        receiver_slot.reshape(1, -1), residual, model_cell.reshape(1, -1),
        *[jnp.asarray(table) for table in tables],
    ]
    out_low, out_high, grad = pl.pallas_call(
        functools.partial(kernel, n),
        out_shape=(
            jax.ShapeDtypeStruct(state_low.shape, jnp.float32),
            jax.ShapeDtypeStruct(state_high.shape, jnp.float32),
            jax.ShapeDtypeStruct((2 * slots // TILE, TILE), jnp.float32),
        ),
        in_specs=[pl.BlockSpec(memory_space=pltpu.SMEM)] + [pl.BlockSpec(memory_space=pl.ANY)] * len(operands),
        out_specs=(vmem, vmem, vmem),
        scratch_shapes=[
            *[pltpu.VMEM(operand.shape, operand.dtype) for operand in operands],
            pltpu.VMEM((64, slots), jnp.float32),
            pltpu.VMEM((3, 64, slots), jnp.float32),
            pltpu.VMEM((128, slots), jnp.float32),
            pltpu.VMEM((3, 128, slots), jnp.float32),
            pltpu.VMEM((4, FACE_ROWS, TILE), jnp.float32),
            pltpu.VMEM((2, side_tiles * ROWS + 8, TILE), jnp.float32),
            pltpu.VMEM((2 * STEPS, 2, side_tiles * ROWS + 8, TILE), jnp.float32),
            pltpu.VMEM((4, 6, ROWS, TILE), jnp.float32),
            pltpu.VMEM((4, 8, TILE), jnp.float32),
            pltpu.VMEM((STEPS, 1, TILE), jnp.float32),
            pltpu.VMEM((1, 2 * slots), jnp.float32),
            pltpu.VMEM((6, 4, 8, TILE), jnp.int32),
            pltpu.VMEM((5, 8, TILE), jnp.float32),
            pltpu.VMEM((5, 8, TILE), jnp.float32),
            pltpu.SemaphoreType.DMA((2 * STEPS, 2)),
            pltpu.SemaphoreType.DMA((2 * STEPS, 2)),
            pltpu.SemaphoreType.DMA((5,)),
            pltpu.SemaphoreType.DMA((5,)),
            pltpu.SemaphoreType.DMA((len(operands),)),
        ],
        compiler_params=pltpu.CompilerParams(
            collective_id=0, has_side_effects=True, vmem_limit_bytes=VMEM_GRANT
        ),
    )(live_count.reshape(1, 2), *operands)
    return out_low, out_high, grad.reshape(-1)


def solution(mesh):
    placed = (
        P("groups", None, "domain"),
        P("groups", None, "domain"),
        P("groups", None, "domain"),
        P("groups", None, "domain"),
        P("domain"),
        P("domain"),
        P("domain"),
        P(None, "domain"),
        P(None, "domain"),
        P(None, "domain"),
        P("domain"),
        P("groups", "domain"),
        P("domain"),
    )
    return jax.shard_map(
        functools.partial(shards, mesh.shape["domain"]),
        mesh=mesh,
        in_specs=placed,
        out_specs=(
            P("groups", None, "domain"),
            P("groups", None, "domain"),
            P(("groups", "domain")),
        ),
        check_vma=False,
    )
```

```python
import functools
import math

import jax
import jax.numpy as jnp
import ml_dtypes
import numpy as np
from jax import lax
from jax.experimental import pallas as pl
from jax.experimental.pallas import tpu as pltpu
from jax.sharding import PartitionSpec as P

STEPS = 2
TIME_STEP = 0.02
SOURCE_WEIGHT = (45.0 / 32.0) ** 3
HIGHEST = lax.Precision.HIGHEST
TILE = 128
ROWS = 24
FACE_ROWS = 6 * ROWS + 8
LOAD_ORDER = tuple(range(21))
VMEM_GRANT = 63 * 1024 * 1024
CENTRE = 62


def gll_points(degree):
    if degree == 3:
        interior = math.sqrt(0.2)
        return np.array([-1.0, -interior, interior, 1.0])
    interior = math.sqrt(3.0 / 7.0)
    return np.array([-1.0, -interior, 0.0, interior, 1.0])


def gll_weights(degree):
    if degree == 3:
        return np.array([1.0 / 6.0, 5.0 / 6.0, 5.0 / 6.0, 1.0 / 6.0])
    return np.array([0.1, 49.0 / 90.0, 32.0 / 45.0, 49.0 / 90.0, 0.1])


def lagrange_table(targets, sources):
    result = np.ones((targets.shape[0], sources.shape[0]))
    for col in range(sources.shape[0]):
        for skip in range(sources.shape[0]):
            if skip != col:
                result[:, col] *= (targets - sources[skip]) / (sources[col] - sources[skip])
    return result


def derivative_table(degree):
    points = gll_points(degree)
    number = points.shape[0]
    barycentric = np.ones(number)
    for col in range(number):
        for skip in range(number):
            if skip != col:
                barycentric[col] /= points[col] - points[skip]
    result = np.zeros((number, number))
    for row in range(number):
        for col in range(number):
            if row != col:
                result[row, col] = barycentric[col] / barycentric[row] / (points[row] - points[col])
        result[row, row] = -np.sum(result[row])
    return result


def halves(matrix):
    high = matrix.astype(ml_dtypes.bfloat16)
    low = (matrix - high.astype(np.float64)).astype(ml_dtypes.bfloat16)
    return high, low


def face_nodes(n, face):
    cube = np.arange(n**3).reshape(n, n, n)
    return np.take(cube, 0 if face % 2 == 0 else n - 1, axis=face // 2).reshape(-1)


def order_tables(degree):
    n = degree + 1
    nodes = 64 if degree == 3 else 128
    lift = 6.0 if degree == 3 else 10.0
    exact = degree == 4
    points, mortar = gll_points(degree), gll_points(4)
    up = np.eye(5) if exact else lagrange_table(mortar, points)
    down = np.eye(5) if exact else lagrange_table(points, mortar)
    up, down = np.kron(up, up), np.kron(down, down)
    sign = np.array([-1.0, 1.0] * 3)
    pressure_trace = np.zeros((FACE_ROWS, nodes))
    velocity_trace = np.zeros((3, FACE_ROWS, nodes))
    place = np.zeros((6, nodes, 25))
    for face in range(6):
        at = face_nodes(n, face)
        rows = np.append(face * ROWS + np.arange(ROWS), 6 * ROWS + face)
        pressure_trace[np.ix_(rows, at)] = up
        velocity_trace[face // 2][np.ix_(rows, at)] = sign[face] * up
        place[face, at] = down
    velocity_trace = np.concatenate(
        [
            np.concatenate([velocity_trace[a, 2 * a * ROWS : 2 * (a + 1) * ROWS], velocity_trace[a, 6 * ROWS :]])
            for a in range(3)
        ]
    ).reshape(3, 2 * ROWS + 8, nodes)
    diff = derivative_table(degree)
    move_v, move_p = [], []
    for a in range(3):
        parts = [np.eye(n)] * 3
        parts[a] = diff
        own = np.zeros((nodes, nodes))
        own[: n**3, : n**3] = np.kron(np.kron(parts[0], parts[1]), parts[2])
        for side in range(2):
            at = face_nodes(n, 2 * a + side)
            own[at, at] += 0.5 * lift * (1 - 2 * side)
        own_hi, own_lo = halves(own)
        for rows, first in ((move_v, -1.0), (move_p, -1.0)):
            second = 1.0 if rows is move_v else -1.0
            other = np.zeros((nodes, 64))
            for side, factor in enumerate((first, second)):
                column = side * ROWS
                other[:, column : column + ROWS] = 0.5 * lift * factor * place[2 * a + side][:, :ROWS]
                other[:, 2 * ROWS + 2 * a + side] = 0.5 * lift * factor * place[2 * a + side][:, ROWS]
            hi, lo = halves(other)
            rows.append(np.concatenate([own_hi, own_hi, own_lo, hi, hi] + ([] if exact else [lo]), 1))

    def spread(matrix):
        hi, lo = halves(matrix)
        return np.concatenate([hi, hi] + ([] if exact else [lo]), -1)

    weights = gll_weights(degree)
    cube = (weights[:, None, None] * weights[None, :, None] * weights[None, None, :]).reshape(-1)
    cube = np.repeat(cube[:, None], 256, 1).astype(np.float32)
    return spread(pressure_trace), spread(velocity_trace), np.stack(move_v), np.stack(move_p), cube


def split(value):
    high = value.astype(jnp.bfloat16)
    return high, (value - high.astype(jnp.float32)).astype(jnp.bfloat16)


def times(matrix, pieces):
    return jnp.dot(matrix, jnp.concatenate(pieces, axis=0), preferred_element_type=jnp.float32)


def picked(index, sources, lasts, start, last):
    lane = index & (TILE - 1)
    tile = index >> 7
    parts = list(start)
    for k, load in sources:
        here = tile == k
        for row in range(ROWS // 8):
            found = jnp.take_along_axis(load(row), lane, axis=1, mode="promise_in_bounds")
            parts[row] = jnp.where(here, found, parts[row])
    sublane = lax.broadcasted_iota(jnp.int32, (8, TILE), 0)
    for first, stride, load in lasts:
        found = jnp.take_along_axis(load(), lane, axis=1, mode="promise_in_bounds")
        last = jnp.where(tile == first + stride * sublane, found, last)
    return parts, last


def kernel(
    n, live, *refs
):
    count = 21
    hbm, outs, vmem = refs[:count], refs[count : count + 3], refs[count + 3 : 2 * count + 3]
    body(n, live, hbm, *vmem, *outs, *refs[2 * count + 3 :])


def body(
    n, live, hbm,
    state_low, state_high, forward_low, forward_high, bulk, buoyancy, stretch, link, send,
    receiver, residual, cell,
    tables_low, tables_high, tv_low, tv_high, mv_low, mv_high, mp_low, mp_high, weights,
    out_low, out_high, grad,
    p_low, v_low, p_high, v_high, table, outgoing, remote, near, near_last, source, terms, wanted, rate, at_lane,
    blocks, arrived, send_sem, recv_sem, gsend_sem, grecv_sem, load_sem,
):
    me = lax.axis_index("domain")
    held = (
        state_low, state_high, forward_low, forward_high, bulk, buoyancy, stretch, link, send,
        receiver, residual, cell,
        tables_low, tables_high, tv_low, tv_high, mv_low, mv_high, mp_low, mp_high, weights,
    )
    loads = [
        pltpu.make_async_copy(source_ref, target, load_sem.at[i])
        for i, (source_ref, target) in enumerate(zip(hbm, held))
    ]
    for i in LOAD_ORDER:
        loads[i].start()
    slots = state_low.shape[2]
    side_tiles = send.shape[1] // TILE
    barrier = pltpu.get_barrier_semaphore()
    count = 0
    for distance in (-2, -1, 1, 2):
        there = me + distance
        exists = jnp.logical_and(there >= 0, there < n)
        count = count + exists.astype(jnp.int32)

        @pl.when(exists)
        def _():
            pl.semaphore_signal(
                barrier, inc=1, device_id={"domain": there}, device_id_type=pl.DeviceIdType.MESH
            )

    @pl.when(me == 0)
    def _():
        remote[:, 0] = jnp.zeros(remote[:, 0].shape, jnp.float32)

    @pl.when(me == n - 1)
    def _():
        remote[:, 1] = jnp.zeros(remote[:, 1].shape, jnp.float32)

    for block in (0, 1, 3, 4):
        origin = me - (block - 2)

        @pl.when(jnp.logical_or(origin < 0, origin >= n))
        def _():
            arrived[block] = jnp.zeros(arrived[block].shape, jnp.float32)

    for load in loads:
        load.wait()
    slot = lax.broadcasted_iota(jnp.int32, (1, slots), 1)
    alive_low = (slot < live[0, 0]).astype(jnp.float32)
    alive_high = (slot < live[0, 1]).astype(jnp.float32)
    p_high[120:128, :] = jnp.zeros((8, slots), jnp.float32)
    for a in range(3):
        v_high[a, 120:128, :] = jnp.zeros((8, slots), jnp.float32)
    rate[...] = forward_high[...].astype(jnp.float32)
    p_low[...] = state_low[0] * alive_low
    for half in range(2):
        lanes = slice(half * TILE, (half + 1) * TILE)
        p_high[0:125, lanes] = state_high[pl.ds(4 * half, 125, stride=8), :] * alive_high[:, lanes]
        for a in range(3):
            v_high[a, 0:125, lanes] = (
                state_high[pl.ds(4 * half + 1 + a, 125, stride=8), :] * alive_high[:, lanes]
            )
    for a in range(3):
        v_low[a] = state_low[1 + a] * alive_low
    stretch_low, stretch_high = stretch[:, :slots], stretch[:, slots:]
    rate_v_low = TIME_STEP * buoyancy[:, :slots] * stretch_low * alive_low
    rate_v_high = TIME_STEP * buoyancy[:, slots:] * stretch_high * alive_high
    rate_p_low = TIME_STEP * bulk[:, :slots] * stretch_low * alive_low
    rate_p_high = TIME_STEP * bulk[:, slots:] * stretch_high * alive_high
    volume_low = stretch_low * stretch_low * stretch_low
    volume_high = stretch_high * stretch_high * stretch_high
    rows = lax.broadcasted_iota(jnp.int32, (TILE, receiver.shape[1]), 0)
    at_slot = (rows == receiver[...]).astype(jnp.float32)
    shared = lax.dot_general(
        jnp.concatenate([residual[...]] * 4, axis=0), at_slot, (((1,), (1,)), ((), ())), precision=HIGHEST,
        preferred_element_type=jnp.float32,
    )
    shared = shared * (
        TIME_STEP * SOURCE_WEIGHT * bulk[:, slots : slots + TILE] * volume_high[:, :TILE]
    )
    for t in range(STEPS):
        source[t] = shared[t : t + 1]
    terms[...] = jnp.zeros(terms.shape, jnp.float32)
    cells = 2 * slots
    relative = cell[...] - (me - 2) * cells
    group = relative >> 7
    group = (group >> 2) * 8 + (group & 3)
    at_lane[...] = jnp.where(
        lax.broadcasted_iota(jnp.int32, (TILE, cells), 0) == (relative & (TILE - 1)), 1.0, 0.0
    ).astype(jnp.bfloat16)
    for face in range(6):
        for quarter in range(4):
            wanted[face, quarter] = jnp.broadcast_to(
                link[face : face + 1, quarter * TILE : (quarter + 1) * TILE], (8, TILE)
            )

    pl.semaphore_wait(barrier, count)

    def copy_down(turn):
        return pltpu.make_async_remote_copy(
            src_ref=outgoing.at[0], dst_ref=remote.at[turn, 1],
            send_sem=send_sem.at[turn, 0], recv_sem=recv_sem.at[turn, 1],
            device_id={"domain": me - 1}, device_id_type=pl.DeviceIdType.MESH,
        )

    def copy_up(turn):
        return pltpu.make_async_remote_copy(
            src_ref=outgoing.at[1], dst_ref=remote.at[turn, 0],
            send_sem=send_sem.at[turn, 1], recv_sem=recv_sem.at[turn, 0],
            device_id={"domain": me + 1}, device_id_type=pl.DeviceIdType.MESH,
        )

    def exchange(turn, traces_low, traces_high):
        for quarter, traces in enumerate((traces_low, traces_low, traces_high, traces_high)):
            table[quarter] = traces[:, (quarter % 2) * TILE : (quarter % 2 + 1) * TILE]

        def load_own(k):
            return lambda row: table[k % 4, (k // 4) * ROWS + 8 * row : (k // 4) * ROWS + 8 * row + 8, :]

        def load_own_last(quarter):
            return lambda: table[quarter, 6 * ROWS :, :]

        lower = [(k, load_own(k)) for k in range(0, 24, 2)]
        lower_last = [(quarter, 4, load_own_last(quarter)) for quarter in (0, 2)]
        zero = jnp.zeros((8, TILE), jnp.float32)
        blank = [zero] * (ROWS // 8)
        sublane = lax.broadcasted_iota(jnp.int32, (8, TILE), 0)
        for way in range(2):

            def pick_out(m, lasts):
                at = pl.multiple_of(m * TILE, TILE)
                index = jnp.broadcast_to(send[way : way + 1, pl.ds(at, TILE)], (8, TILE))
                parts, last = picked(index, lower, lower_last, blank, zero)
                for row in range(ROWS // 8):
                    into = pl.multiple_of(m * ROWS + 8 * row, 8)
                    outgoing[way, pl.ds(into, 8), :] = parts[row]
                return jnp.where(sublane == m, jnp.sum(last, axis=0, keepdims=True), lasts)

            outgoing[way, side_tiles * ROWS :, :] = lax.fori_loop(0, side_tiles, pick_out, zero)
            if way == 0:

                @pl.when(me > 0)
                def _():
                    copy_down(turn).start()
            else:

                @pl.when(me < n - 1)
                def _():
                    copy_up(turn).start()

        own = [(k, load_own(k)) for k in range(24)]
        own_last = [(quarter, 4, load_own_last(quarter)) for quarter in range(4)]

        def pick_own(face, lasts):
            result = []
            for quarter in range(4):
                parts, last = picked(wanted[face, quarter], own, own_last, blank, zero)
                for row in range(ROWS // 8):
                    near[quarter, face, 8 * row : 8 * row + 8, :] = parts[row]
                result.append(
                    jnp.where(sublane == face, jnp.sum(last, axis=0, keepdims=True), lasts[quarter])
                )
            return tuple(result)

        lasts = lax.fori_loop(0, 6, pick_own, (zero,) * 4)
        for quarter in range(4):
            near_last[quarter] = lasts[quarter]

        @pl.when(me > 0)
        def _():
            copy_down(turn).wait_send()
            copy_up(turn).wait_recv()

        @pl.when(me < n - 1)
        def _():
            copy_up(turn).wait_send()
            copy_down(turn).wait_recv()

        def load_far(m):
            way, first = m // side_tiles, (m % side_tiles) * ROWS
            return lambda row: remote[turn, way, first + 8 * row : first + 8 * row + 8, :]

        def load_far_last(way):
            return lambda: remote[turn, way, side_tiles * ROWS :, :]

        far = [(24 + m, load_far(m)) for m in range(2 * side_tiles)]
        far_last = [(24 + way * side_tiles, 1, load_far_last(way)) for way in range(2)]

        def pick_far(face, lasts):
            result = []
            for place, quarter in enumerate((0, 2)):
                start = [near[quarter, face, 8 * row : 8 * row + 8, :] for row in range(ROWS // 8)]
                parts, last = picked(wanted[face, quarter], far, far_last, start, zero)
                for row in range(ROWS // 8):
                    near[quarter, face, 8 * row : 8 * row + 8, :] = parts[row]
                result.append(
                    jnp.where(sublane == face, jnp.sum(last, axis=0, keepdims=True), lasts[place])
                )
            return tuple(result)

        lasts = lax.fori_loop(0, 6, pick_far, (zero,) * 2)
        near_last[0] += lasts[0]
        near_last[2] += lasts[1]

    def neighbours(a):
        pieces = []
        for order in range(2):
            sides = []
            for half in range(2):
                quarter = 2 * order + half
                sides.append(
                    jnp.concatenate(
                        [
                            near[quarter, 2 * a],
                            near[quarter, 2 * a + 1],
                            near_last[quarter],
                            jnp.zeros((8, TILE), jnp.float32),
                        ],
                        axis=0,
                    )
                )
            pieces.append(split(jnp.concatenate(sides, axis=1)))
        (low_hi, low_lo), (high_hi, high_lo) = pieces
        return [low_hi, low_lo, low_hi], [high_hi, high_lo]

    def joined(traces):
        faces = [trace[: 2 * ROWS] for trace in traces]
        return jnp.concatenate(faces + [sum(trace[2 * ROWS :] for trace in traces)], axis=0)

    def step(t, carry):
        low_hi, low_lo = split(p_low[...])
        high_hi, high_lo = split(p_high[...])
        exchange(
            2 * t,
            times(tables_low[...], [low_hi, low_lo, low_hi]),
            times(tables_high[...], [high_hi, high_lo]),
        )
        traces_low, traces_high = [], []
        for a in range(3):
            from_low, from_high = neighbours(a)
            pl_hi, pl_lo = split(p_low[...])
            ph_hi, ph_lo = split(p_high[...])
            new_low = v_low[a] - rate_v_low * times(mv_low[a], [pl_hi, pl_lo, pl_hi] + from_low)
            new_high = v_high[a] - rate_v_high * times(mv_high[a], [ph_hi, ph_lo, ph_hi] + from_high)
            v_low[a] = new_low
            v_high[a] = new_high
            low_hi, low_lo = split(new_low)
            high_hi, high_lo = split(new_high)
            traces_low.append(times(tv_low[a], [low_hi, low_lo, low_hi]))
            traces_high.append(times(tv_high[a], [high_hi, high_lo]))
        exchange(2 * t + 1, joined(traces_low), joined(traces_high))
        total_low, total_high = 0.0, 0.0
        for a in range(3):
            from_low, from_high = neighbours(a)
            low_hi, low_lo = split(v_low[a])
            high_hi, high_lo = split(v_high[a])
            total_low = total_low + times(mp_low[a], [low_hi, low_lo, low_hi] + from_low)
            total_high = total_high + times(mp_high[a], [high_hi, high_lo, high_hi] + from_high)
        p_low[...] = p_low[...] - rate_p_low * total_low
        p_high[...] = p_high[...] - rate_p_high * total_high
        p_high[CENTRE : CENTRE + 1, :TILE] = (
            p_high[CENTRE : CENTRE + 1, :TILE] + source[t]
        )
        weighted_low = weights[0:64] * forward_low[t].astype(jnp.float32) * p_low[...]
        forward_now = jnp.concatenate(
            [rate[pl.ds(2 * half + t, 125, stride=4), :] for half in range(2)], axis=1
        )
        weighted_high = weights[64:189] * forward_now * p_high[0:125, :]
        terms[:, :slots] += jnp.sum(weighted_low, axis=0, keepdims=True) / volume_low
        terms[:, slots:] += jnp.sum(weighted_high, axis=0, keepdims=True) / volume_high
        return carry

    lax.fori_loop(0, STEPS, step, 0)

    placed = jnp.where(
        lax.broadcasted_iota(jnp.int32, (40, cells), 0) == group, terms[...], 0.0
    )
    pieces = []
    for _ in range(3):
        pieces.append(placed.astype(jnp.bfloat16).astype(jnp.float32))
        placed = placed - pieces[-1]
    pieces.append(jnp.zeros((8, cells), jnp.float32))
    window = lax.dot_general(
        jnp.concatenate(pieces, axis=0).astype(jnp.bfloat16), at_lane[...],
        (((1,), (1,)), ((), ())), preferred_element_type=jnp.float32,
    )
    window = window[0:40] + window[40:80] + window[80:120]
    blocks[...] = window.reshape(5, 8, TILE)

    def gradient_copy(block):
        return pltpu.make_async_remote_copy(
            src_ref=blocks.at[block], dst_ref=arrived.at[block],
            send_sem=gsend_sem.at[block], recv_sem=grecv_sem.at[block],
            device_id={"domain": me + (block - 2)}, device_id_type=pl.DeviceIdType.MESH,
        )

    for block in (0, 4, 1, 3):
        there = me + (block - 2)

        @pl.when(jnp.logical_and(there >= 0, there < n))
        def _():
            gradient_copy(block).start()

    out_low[0] = p_low[...]
    for a in range(3):
        out_low[1 + a] = v_low[a]
    for half in range(2):
        lanes = slice(half * TILE, (half + 1) * TILE)
        out_high[pl.ds(4 * half, 125, stride=8), :] = p_high[0:125, lanes]
        for a in range(3):
            out_high[pl.ds(4 * half + 1 + a, 125, stride=8), :] = v_high[a, 0:125, lanes]
    for block in (0, 4, 1, 3):
        there = me + (block - 2)
        origin = me - (block - 2)

        @pl.when(jnp.logical_and(there >= 0, there < n))
        def _():
            gradient_copy(block).wait_send()

        @pl.when(jnp.logical_and(origin >= 0, origin < n))
        def _():
            gradient_copy(block).wait_recv()

    total = blocks[2]
    for block in (0, 1, 3, 4):
        total = total + arrived[block]
    grad[...] = total[:4]


def node_rows(values):
    lead, nodes, slots = values.shape
    return values.reshape(lead, nodes, slots // TILE, TILE).transpose(1, 2, 0, 3).reshape(-1, TILE)


def shards(n, state_low, state_high, forward_low, forward_high, bulk_modulus, buoyancy, stretch,
           live_count, face_link, send_faces, receiver_slot, residual, model_cell):
    tp_low, tv_low, mv_low, mp_low, weight_low = order_tables(3)
    tp_high, tv_high, mv_high, mp_high, weight_high = order_tables(4)
    tables = [tp_low, tp_high, tv_low, tv_high, mv_low, mv_high, mp_low, mp_high, np.concatenate([weight_low, weight_high])]
    slots = state_low.shape[2]
    side_tiles = send_faces.shape[1] // TILE
    vmem = pl.BlockSpec(memory_space=pltpu.VMEM)
    operands = [
        state_low, node_rows(state_high), forward_low, node_rows(forward_high), bulk_modulus.reshape(1, -1),
        buoyancy.reshape(1, -1), stretch.reshape(1, -1), face_link, send_faces,
        receiver_slot.reshape(1, -1), residual, model_cell.reshape(1, -1),
        *[jnp.asarray(table) for table in tables],
    ]
    out_low, out_high, grad = pl.pallas_call(
        functools.partial(kernel, n),
        out_shape=(
            jax.ShapeDtypeStruct(state_low.shape, jnp.float32),
            jax.ShapeDtypeStruct((1000, TILE), jnp.float32),
            jax.ShapeDtypeStruct((2 * slots // TILE, TILE), jnp.float32),
        ),
        in_specs=[pl.BlockSpec(memory_space=pltpu.SMEM)] + [pl.BlockSpec(memory_space=pl.ANY)] * len(operands),
        out_specs=(vmem, vmem, vmem),
        scratch_shapes=[
            *[pltpu.VMEM(operand.shape, operand.dtype) for operand in operands],
            pltpu.VMEM((64, slots), jnp.float32),
            pltpu.VMEM((3, 64, slots), jnp.float32),
            pltpu.VMEM((128, slots), jnp.float32),
            pltpu.VMEM((3, 128, slots), jnp.float32),
            pltpu.VMEM((4, FACE_ROWS, TILE), jnp.float32),
            pltpu.VMEM((2, side_tiles * ROWS + 8, TILE), jnp.float32),
            pltpu.VMEM((2 * STEPS, 2, side_tiles * ROWS + 8, TILE), jnp.float32),
            pltpu.VMEM((4, 6, ROWS, TILE), jnp.float32),
            pltpu.VMEM((4, 8, TILE), jnp.float32),
            pltpu.VMEM((STEPS, 1, TILE), jnp.float32),
            pltpu.VMEM((1, 2 * slots), jnp.float32),
            pltpu.VMEM((6, 4, 8, TILE), jnp.int32),
            pltpu.VMEM((500, TILE), jnp.float32),
            pltpu.VMEM((TILE, 2 * slots), jnp.bfloat16),
            pltpu.VMEM((5, 8, TILE), jnp.float32),
            pltpu.VMEM((5, 8, TILE), jnp.float32),
            pltpu.SemaphoreType.DMA((2 * STEPS, 2)),
            pltpu.SemaphoreType.DMA((2 * STEPS, 2)),
            pltpu.SemaphoreType.DMA((5,)),
            pltpu.SemaphoreType.DMA((5,)),
            pltpu.SemaphoreType.DMA((len(operands),)),
        ],
        compiler_params=pltpu.CompilerParams(
            collective_id=0, has_side_effects=True, vmem_limit_bytes=VMEM_GRANT
        ),
    )(live_count.reshape(1, 2), *operands)
    out_high = out_high.reshape(125, 2, 4, TILE).transpose(2, 0, 1, 3).reshape(state_high.shape)
    return out_low, out_high, grad.reshape(-1)


def solution(mesh):
    placed = (
        P("groups", None, "domain"),
        P("groups", None, "domain"),
        P("groups", None, "domain"),
        P("groups", None, "domain"),
        P("domain"),
        P("domain"),
        P("domain"),
        P(None, "domain"),
        P(None, "domain"),
        P(None, "domain"),
        P("domain"),
        P("groups", "domain"),
        P("domain"),
    )
    return jax.shard_map(
        functools.partial(shards, mesh.shape["domain"]),
        mesh=mesh,
        in_specs=placed,
        out_specs=(
            P("groups", None, "domain"),
            P("groups", None, "domain"),
            P(("groups", "domain")),
        ),
        check_vma=False,
    )
```

```python
import functools
import math

import jax
import jax.numpy as jnp
import ml_dtypes
import numpy as np
from jax import lax
from jax.experimental import pallas as pl
from jax.experimental.pallas import tpu as pltpu
from jax.sharding import PartitionSpec as P

STEPS = 2
TIME_STEP = 0.02
SOURCE_WEIGHT = (45.0 / 32.0) ** 3
HIGHEST = lax.Precision.HIGHEST
TILE = 128
ROWS = 24
FACE_ROWS = 6 * ROWS + 8
LOAD_ORDER = tuple(range(21))
VMEM_GRANT = 63 * 1024 * 1024
CENTRE = 62


def gll_points(degree):
    if degree == 3:
        interior = math.sqrt(0.2)
        return np.array([-1.0, -interior, interior, 1.0])
    interior = math.sqrt(3.0 / 7.0)
    return np.array([-1.0, -interior, 0.0, interior, 1.0])


def gll_weights(degree):
    if degree == 3:
        return np.array([1.0 / 6.0, 5.0 / 6.0, 5.0 / 6.0, 1.0 / 6.0])
    return np.array([0.1, 49.0 / 90.0, 32.0 / 45.0, 49.0 / 90.0, 0.1])


def lagrange_table(targets, sources):
    result = np.ones((targets.shape[0], sources.shape[0]))
    for col in range(sources.shape[0]):
        for skip in range(sources.shape[0]):
            if skip != col:
                result[:, col] *= (targets - sources[skip]) / (sources[col] - sources[skip])
    return result


def derivative_table(degree):
    points = gll_points(degree)
    number = points.shape[0]
    barycentric = np.ones(number)
    for col in range(number):
        for skip in range(number):
            if skip != col:
                barycentric[col] /= points[col] - points[skip]
    result = np.zeros((number, number))
    for row in range(number):
        for col in range(number):
            if row != col:
                result[row, col] = barycentric[col] / barycentric[row] / (points[row] - points[col])
        result[row, row] = -np.sum(result[row])
    return result


def halves(matrix):
    high = matrix.astype(ml_dtypes.bfloat16)
    low = (matrix - high.astype(np.float64)).astype(ml_dtypes.bfloat16)
    return high, low


def face_nodes(n, face):
    cube = np.arange(n**3).reshape(n, n, n)
    return np.take(cube, 0 if face % 2 == 0 else n - 1, axis=face // 2).reshape(-1)


def order_tables(degree):
    n = degree + 1
    nodes = 64 if degree == 3 else 128
    lift = 6.0 if degree == 3 else 10.0
    exact = degree == 4
    points, mortar = gll_points(degree), gll_points(4)
    up = np.eye(5) if exact else lagrange_table(mortar, points)
    down = np.eye(5) if exact else lagrange_table(points, mortar)
    up, down = np.kron(up, up), np.kron(down, down)
    sign = np.array([-1.0, 1.0] * 3)
    pressure_trace = np.zeros((FACE_ROWS, nodes))
    velocity_trace = np.zeros((3, FACE_ROWS, nodes))
    place = np.zeros((6, nodes, 25))
    for face in range(6):
        at = face_nodes(n, face)
        rows = np.append(face * ROWS + np.arange(ROWS), 6 * ROWS + face)
        pressure_trace[np.ix_(rows, at)] = up
        velocity_trace[face // 2][np.ix_(rows, at)] = sign[face] * up
        place[face, at] = down
    velocity_trace = np.concatenate(
        [
            np.concatenate([velocity_trace[a, 2 * a * ROWS : 2 * (a + 1) * ROWS], velocity_trace[a, 6 * ROWS :]])
            for a in range(3)
        ]
    ).reshape(3, 2 * ROWS + 8, nodes)
    diff = derivative_table(degree)
    move_v, move_p = [], []
    for a in range(3):
        parts = [np.eye(n)] * 3
        parts[a] = diff
        own = np.zeros((nodes, nodes))
        own[: n**3, : n**3] = np.kron(np.kron(parts[0], parts[1]), parts[2])
        for side in range(2):
            at = face_nodes(n, 2 * a + side)
            own[at, at] += 0.5 * lift * (1 - 2 * side)
        own_hi, own_lo = halves(own)
        for rows, first in ((move_v, -1.0), (move_p, -1.0)):
            second = 1.0 if rows is move_v else -1.0
            other = np.zeros((nodes, 64))
            for side, factor in enumerate((first, second)):
                column = side * ROWS
                other[:, column : column + ROWS] = 0.5 * lift * factor * place[2 * a + side][:, :ROWS]
                other[:, 2 * ROWS + 2 * a + side] = 0.5 * lift * factor * place[2 * a + side][:, ROWS]
            hi, lo = halves(other)
            rows.append(np.concatenate([own_hi, own_hi, own_lo, hi, hi] + ([] if exact else [lo]), 1))

    def spread(matrix):
        hi, lo = halves(matrix)
        return np.concatenate([hi, hi] + ([] if exact else [lo]), -1)

    weights = gll_weights(degree)
    cube = (weights[:, None, None] * weights[None, :, None] * weights[None, None, :]).reshape(-1)
    cube = np.repeat(cube[:, None], 256, 1).astype(np.float32)
    return spread(pressure_trace), spread(velocity_trace), np.stack(move_v), np.stack(move_p), cube


def split(value):
    high = value.astype(jnp.bfloat16)
    return high, (value - high.astype(jnp.float32)).astype(jnp.bfloat16)


def times(matrix, pieces):
    return jnp.dot(matrix, jnp.concatenate(pieces, axis=0), preferred_element_type=jnp.float32)


def picked(index, sources, lasts, start, last):
    lane = index & (TILE - 1)
    tile = index >> 7
    parts = list(start)
    for k, load in sources:
        here = tile == k
        for row in range(ROWS // 8):
            found = jnp.take_along_axis(load(row), lane, axis=1, mode="promise_in_bounds")
            parts[row] = jnp.where(here, found, parts[row])
    sublane = lax.broadcasted_iota(jnp.int32, (8, TILE), 0)
    for first, stride, load in lasts:
        found = jnp.take_along_axis(load(), lane, axis=1, mode="promise_in_bounds")
        last = jnp.where(tile == first + stride * sublane, found, last)
    return parts, last


def kernel(
    n, live, *refs
):
    count = 21
    hbm, outs, vmem = refs[:count], refs[count : count + 3], refs[count + 3 : 2 * count + 3]
    body(n, live, hbm, outs[:2], *vmem, outs[2], *refs[2 * count + 3 :])


def body(
    n, live, hbm, final,
    state_low, state_high, forward_low, forward_high, bulk, buoyancy, stretch, link, send,
    receiver, residual, cell,
    tables_low, tables_high, tv_low, tv_high, mv_low, mv_high, mp_low, mp_high, weights,
    grad, out_low, out_high,
    p_low, v_low, p_high, v_high, table, outgoing, remote, near, near_last, source, terms, wanted, rate, at_lane,
    blocks, arrived, send_sem, recv_sem, gsend_sem, grecv_sem, load_sem, store_sem,
):
    me = lax.axis_index("domain")
    held = (
        state_low, state_high, forward_low, forward_high, bulk, buoyancy, stretch, link, send,
        receiver, residual, cell,
        tables_low, tables_high, tv_low, tv_high, mv_low, mv_high, mp_low, mp_high, weights,
    )
    loads = [
        pltpu.make_async_copy(source_ref, target, load_sem.at[i])
        for i, (source_ref, target) in enumerate(zip(hbm, held))
    ]
    for i in LOAD_ORDER:
        loads[i].start()
    slots = state_low.shape[2]
    side_tiles = send.shape[1] // TILE
    barrier = pltpu.get_barrier_semaphore()
    count = 0
    for distance in (-2, -1, 1, 2):
        there = me + distance
        exists = jnp.logical_and(there >= 0, there < n)
        count = count + exists.astype(jnp.int32)

        @pl.when(exists)
        def _():
            pl.semaphore_signal(
                barrier, inc=1, device_id={"domain": there}, device_id_type=pl.DeviceIdType.MESH
            )

    @pl.when(me == 0)
    def _():
        remote[:, 0] = jnp.zeros(remote[:, 0].shape, jnp.float32)

    @pl.when(me == n - 1)
    def _():
        remote[:, 1] = jnp.zeros(remote[:, 1].shape, jnp.float32)

    for block in (0, 1, 3, 4):
        origin = me - (block - 2)

        @pl.when(jnp.logical_or(origin < 0, origin >= n))
        def _():
            arrived[block] = jnp.zeros(arrived[block].shape, jnp.float32)

    for load in loads:
        load.wait()
    slot = lax.broadcasted_iota(jnp.int32, (1, slots), 1)
    alive_low = (slot < live[0, 0]).astype(jnp.float32)
    alive_high = (slot < live[0, 1]).astype(jnp.float32)
    p_high[120:128, :] = jnp.zeros((8, slots), jnp.float32)
    for a in range(3):
        v_high[a, 120:128, :] = jnp.zeros((8, slots), jnp.float32)
    rate[...] = forward_high[...].astype(jnp.float32).reshape(rate.shape)
    p_low[...] = state_low[0] * alive_low
    for half in range(2):
        lanes = slice(half * TILE, (half + 1) * TILE)
        p_high[0:125, lanes] = state_high[pl.ds(4 * half, 125, stride=8), :] * alive_high[:, lanes]
        for a in range(3):
            v_high[a, 0:125, lanes] = (
                state_high[pl.ds(4 * half + 1 + a, 125, stride=8), :] * alive_high[:, lanes]
            )
    for a in range(3):
        v_low[a] = state_low[1 + a] * alive_low
    stretch_low, stretch_high = stretch[:, :slots], stretch[:, slots:]
    rate_v_low = TIME_STEP * buoyancy[:, :slots] * stretch_low * alive_low
    rate_v_high = TIME_STEP * buoyancy[:, slots:] * stretch_high * alive_high
    rate_p_low = TIME_STEP * bulk[:, :slots] * stretch_low * alive_low
    rate_p_high = TIME_STEP * bulk[:, slots:] * stretch_high * alive_high
    volume_low = stretch_low * stretch_low * stretch_low
    volume_high = stretch_high * stretch_high * stretch_high
    rows = lax.broadcasted_iota(jnp.int32, (TILE, receiver.shape[1]), 0)
    at_slot = (rows == receiver[...]).astype(jnp.float32)
    shared = lax.dot_general(
        jnp.concatenate([residual[...]] * 4, axis=0), at_slot, (((1,), (1,)), ((), ())), precision=HIGHEST,
        preferred_element_type=jnp.float32,
    )
    shared = shared * (
        TIME_STEP * SOURCE_WEIGHT * bulk[:, slots : slots + TILE] * volume_high[:, :TILE]
    )
    for t in range(STEPS):
        source[t] = shared[t : t + 1]
    terms[...] = jnp.zeros(terms.shape, jnp.float32)
    cells = 2 * slots
    relative = cell[...] - (me - 2) * cells
    group = relative >> 7
    group = (group >> 2) * 8 + (group & 3)
    at_lane[...] = jnp.where(
        lax.broadcasted_iota(jnp.int32, (TILE, cells), 0) == (relative & (TILE - 1)), 1.0, 0.0
    ).astype(jnp.bfloat16)
    for face in range(6):
        for quarter in range(4):
            wanted[face, quarter] = jnp.broadcast_to(
                link[face : face + 1, quarter * TILE : (quarter + 1) * TILE], (8, TILE)
            )

    pl.semaphore_wait(barrier, count)

    def copy_down(turn):
        return pltpu.make_async_remote_copy(
            src_ref=outgoing.at[0], dst_ref=remote.at[turn, 1],
            send_sem=send_sem.at[turn, 0], recv_sem=recv_sem.at[turn, 1],
            device_id={"domain": me - 1}, device_id_type=pl.DeviceIdType.MESH,
        )

    def copy_up(turn):
        return pltpu.make_async_remote_copy(
            src_ref=outgoing.at[1], dst_ref=remote.at[turn, 0],
            send_sem=send_sem.at[turn, 1], recv_sem=recv_sem.at[turn, 0],
            device_id={"domain": me + 1}, device_id_type=pl.DeviceIdType.MESH,
        )

    def exchange(turn, traces_low, traces_high):
        for quarter, traces in enumerate((traces_low, traces_low, traces_high, traces_high)):
            table[quarter] = traces[:, (quarter % 2) * TILE : (quarter % 2 + 1) * TILE]

        def load_own(k):
            return lambda row: table[k % 4, (k // 4) * ROWS + 8 * row : (k // 4) * ROWS + 8 * row + 8, :]

        def load_own_last(quarter):
            return lambda: table[quarter, 6 * ROWS :, :]

        lower = [(k, load_own(k)) for k in range(0, 24, 2)]
        lower_last = [(quarter, 4, load_own_last(quarter)) for quarter in (0, 2)]
        zero = jnp.zeros((8, TILE), jnp.float32)
        blank = [zero] * (ROWS // 8)
        sublane = lax.broadcasted_iota(jnp.int32, (8, TILE), 0)
        for way in range(2):

            def pick_out(m, lasts):
                at = pl.multiple_of(m * TILE, TILE)
                index = jnp.broadcast_to(send[way : way + 1, pl.ds(at, TILE)], (8, TILE))
                parts, last = picked(index, lower, lower_last, blank, zero)
                for row in range(ROWS // 8):
                    into = pl.multiple_of(m * ROWS + 8 * row, 8)
                    outgoing[way, pl.ds(into, 8), :] = parts[row]
                return jnp.where(sublane == m, jnp.sum(last, axis=0, keepdims=True), lasts)

            outgoing[way, side_tiles * ROWS :, :] = lax.fori_loop(0, side_tiles, pick_out, zero)
            if way == 0:

                @pl.when(me > 0)
                def _():
                    copy_down(turn).start()
            else:

                @pl.when(me < n - 1)
                def _():
                    copy_up(turn).start()

        own = [(k, load_own(k)) for k in range(24)]
        own_last = [(quarter, 4, load_own_last(quarter)) for quarter in range(4)]

        def pick_own(face, lasts):
            result = []
            for quarter in range(4):
                parts, last = picked(wanted[face, quarter], own, own_last, blank, zero)
                for row in range(ROWS // 8):
                    near[quarter, face, 8 * row : 8 * row + 8, :] = parts[row]
                result.append(
                    jnp.where(sublane == face, jnp.sum(last, axis=0, keepdims=True), lasts[quarter])
                )
            return tuple(result)

        lasts = lax.fori_loop(0, 6, pick_own, (zero,) * 4)
        for quarter in range(4):
            near_last[quarter] = lasts[quarter]

        @pl.when(me > 0)
        def _():
            copy_down(turn).wait_send()
            copy_up(turn).wait_recv()

        @pl.when(me < n - 1)
        def _():
            copy_up(turn).wait_send()
            copy_down(turn).wait_recv()

        def load_far(m):
            way, first = m // side_tiles, (m % side_tiles) * ROWS
            return lambda row: remote[turn, way, first + 8 * row : first + 8 * row + 8, :]

        def load_far_last(way):
            return lambda: remote[turn, way, side_tiles * ROWS :, :]

        far = [(24 + m, load_far(m)) for m in range(2 * side_tiles)]
        far_last = [(24 + way * side_tiles, 1, load_far_last(way)) for way in range(2)]

        def pick_far(face, lasts):
            result = []
            for place, quarter in enumerate((0, 2)):
                start = [near[quarter, face, 8 * row : 8 * row + 8, :] for row in range(ROWS // 8)]
                parts, last = picked(wanted[face, quarter], far, far_last, start, zero)
                for row in range(ROWS // 8):
                    near[quarter, face, 8 * row : 8 * row + 8, :] = parts[row]
                result.append(
                    jnp.where(sublane == face, jnp.sum(last, axis=0, keepdims=True), lasts[place])
                )
            return tuple(result)

        lasts = lax.fori_loop(0, 6, pick_far, (zero,) * 2)
        near_last[0] += lasts[0]
        near_last[2] += lasts[1]

    def neighbours(a):
        pieces = []
        for order in range(2):
            sides = []
            for half in range(2):
                quarter = 2 * order + half
                sides.append(
                    jnp.concatenate(
                        [
                            near[quarter, 2 * a],
                            near[quarter, 2 * a + 1],
                            near_last[quarter],
                            jnp.zeros((8, TILE), jnp.float32),
                        ],
                        axis=0,
                    )
                )
            pieces.append(split(jnp.concatenate(sides, axis=1)))
        (low_hi, low_lo), (high_hi, high_lo) = pieces
        return [low_hi, low_lo, low_hi], [high_hi, high_lo]

    def joined(traces):
        faces = [trace[: 2 * ROWS] for trace in traces]
        return jnp.concatenate(faces + [sum(trace[2 * ROWS :] for trace in traces)], axis=0)

    def step(t, carry):
        low_hi, low_lo = split(p_low[...])
        high_hi, high_lo = split(p_high[...])
        exchange(
            2 * t,
            times(tables_low[...], [low_hi, low_lo, low_hi]),
            times(tables_high[...], [high_hi, high_lo]),
        )
        traces_low, traces_high = [], []
        pl_hi, pl_lo = split(p_low[...])
        ph_hi, ph_lo = split(p_high[...])
        for a in range(3):
            from_low, from_high = neighbours(a)
            new_low = v_low[a] - rate_v_low * times(mv_low[a], [pl_hi, pl_lo, pl_hi] + from_low)
            new_high = v_high[a] - rate_v_high * times(mv_high[a], [ph_hi, ph_lo, ph_hi] + from_high)
            v_low[a] = new_low
            v_high[a] = new_high
            low_hi, low_lo = split(new_low)
            high_hi, high_lo = split(new_high)
            traces_low.append(times(tv_low[a], [low_hi, low_lo, low_hi]))
            traces_high.append(times(tv_high[a], [high_hi, high_lo]))
        exchange(2 * t + 1, joined(traces_low), joined(traces_high))
        total_low, total_high = 0.0, 0.0
        for a in range(3):
            from_low, from_high = neighbours(a)
            low_hi, low_lo = split(v_low[a])
            high_hi, high_lo = split(v_high[a])
            total_low = total_low + times(mp_low[a], [low_hi, low_lo, low_hi] + from_low)
            total_high = total_high + times(mp_high[a], [high_hi, high_lo, high_hi] + from_high)
        p_low[...] = p_low[...] - rate_p_low * total_low
        p_high[...] = p_high[...] - rate_p_high * total_high
        p_high[CENTRE : CENTRE + 1, :TILE] = (
            p_high[CENTRE : CENTRE + 1, :TILE] + source[t]
        )
        weighted_low = weights[0:64] * forward_low[t].astype(jnp.float32) * p_low[...]
        forward_now = jnp.concatenate(
            [rate[pl.ds(2 * half + t, 125, stride=4), :] for half in range(2)], axis=1
        )
        weighted_high = weights[64:189] * forward_now * p_high[0:125, :]
        terms[:, :slots] += jnp.sum(weighted_low, axis=0, keepdims=True) / volume_low
        terms[:, slots:] += jnp.sum(weighted_high, axis=0, keepdims=True) / volume_high
        return carry

    lax.fori_loop(0, STEPS, step, 0)

    placed = jnp.where(
        lax.broadcasted_iota(jnp.int32, (40, cells), 0) == group, terms[...], 0.0
    )
    pieces = []
    for _ in range(3):
        pieces.append(placed.astype(jnp.bfloat16).astype(jnp.float32))
        placed = placed - pieces[-1]
    pieces.append(jnp.zeros((8, cells), jnp.float32))
    window = lax.dot_general(
        jnp.concatenate(pieces, axis=0).astype(jnp.bfloat16), at_lane[...],
        (((1,), (1,)), ((), ())), preferred_element_type=jnp.float32,
    )
    window = window[0:40] + window[40:80] + window[80:120]
    blocks[...] = window.reshape(5, 8, TILE)

    def gradient_copy(block):
        return pltpu.make_async_remote_copy(
            src_ref=blocks.at[block], dst_ref=arrived.at[block],
            send_sem=gsend_sem.at[block], recv_sem=grecv_sem.at[block],
            device_id={"domain": me + (block - 2)}, device_id_type=pl.DeviceIdType.MESH,
        )

    for block in (0, 4, 1, 3):
        there = me + (block - 2)

        @pl.when(jnp.logical_and(there >= 0, there < n))
        def _():
            gradient_copy(block).start()

    out_low[0] = p_low[...]
    for a in range(3):
        out_low[1 + a] = v_low[a]
    stores = [
        pltpu.make_async_copy(out_low, final[0], store_sem.at[0]),
        pltpu.make_async_copy(out_high, final[1], store_sem.at[1]),
    ]
    stores[0].start()
    for half in range(2):
        lanes = slice(half * TILE, (half + 1) * TILE)
        out_high[pl.ds(4 * half, 125, stride=8), :] = p_high[0:125, lanes]
        for a in range(3):
            out_high[pl.ds(4 * half + 1 + a, 125, stride=8), :] = v_high[a, 0:125, lanes]
    stores[1].start()
    for block in (0, 4, 1, 3):
        there = me + (block - 2)
        origin = me - (block - 2)

        @pl.when(jnp.logical_and(there >= 0, there < n))
        def _():
            gradient_copy(block).wait_send()

        @pl.when(jnp.logical_and(origin >= 0, origin < n))
        def _():
            gradient_copy(block).wait_recv()

    total = blocks[2]
    for block in (0, 1, 3, 4):
        total = total + arrived[block]
    grad[...] = total[:4]
    for store in stores:
        store.wait()


def node_rows(values):
    lead, nodes, slots = values.shape
    return values.reshape(lead, nodes, slots // TILE, TILE).transpose(1, 2, 0, 3).reshape(-1, TILE)


def shards(n, state_low, state_high, forward_low, forward_high, bulk_modulus, buoyancy, stretch,
           live_count, face_link, send_faces, receiver_slot, residual, model_cell):
    tp_low, tv_low, mv_low, mp_low, weight_low = order_tables(3)
    tp_high, tv_high, mv_high, mp_high, weight_high = order_tables(4)
    tables = [tp_low, tp_high, tv_low, tv_high, mv_low, mv_high, mp_low, mp_high, np.concatenate([weight_low, weight_high])]
    slots = state_low.shape[2]
    side_tiles = send_faces.shape[1] // TILE
    vmem = pl.BlockSpec(memory_space=pltpu.VMEM)
    operands = [
        state_low, node_rows(state_high), forward_low, node_rows(forward_high).reshape(-1, STEPS, TILE), bulk_modulus.reshape(1, -1),
        buoyancy.reshape(1, -1), stretch.reshape(1, -1), face_link, send_faces,
        receiver_slot.reshape(1, -1), residual, model_cell.reshape(1, -1),
        *[jnp.asarray(table) for table in tables],
    ]
    out_low, out_high, grad = pl.pallas_call(
        functools.partial(kernel, n),
        out_shape=(
            jax.ShapeDtypeStruct(state_low.shape, jnp.float32),
            jax.ShapeDtypeStruct((1000, TILE), jnp.float32),
            jax.ShapeDtypeStruct((2 * slots // TILE, TILE), jnp.float32),
        ),
        in_specs=[pl.BlockSpec(memory_space=pltpu.SMEM)] + [pl.BlockSpec(memory_space=pl.ANY)] * len(operands),
        out_specs=(pl.BlockSpec(memory_space=pl.ANY), pl.BlockSpec(memory_space=pl.ANY), vmem),
        scratch_shapes=[
            *[pltpu.VMEM(operand.shape, operand.dtype) for operand in operands],
            pltpu.VMEM(state_low.shape, jnp.float32),
            pltpu.VMEM((1000, TILE), jnp.float32),
            pltpu.VMEM((64, slots), jnp.float32),
            pltpu.VMEM((3, 64, slots), jnp.float32),
            pltpu.VMEM((128, slots), jnp.float32),
            pltpu.VMEM((3, 128, slots), jnp.float32),
            pltpu.VMEM((4, FACE_ROWS, TILE), jnp.float32),
            pltpu.VMEM((2, side_tiles * ROWS + 8, TILE), jnp.float32),
            pltpu.VMEM((2 * STEPS, 2, side_tiles * ROWS + 8, TILE), jnp.float32),
            pltpu.VMEM((4, 6, ROWS, TILE), jnp.float32),
            pltpu.VMEM((4, 8, TILE), jnp.float32),
            pltpu.VMEM((STEPS, 1, TILE), jnp.float32),
            pltpu.VMEM((1, 2 * slots), jnp.float32),
            pltpu.VMEM((6, 4, 8, TILE), jnp.int32),
            pltpu.VMEM((500, TILE), jnp.float32),
            pltpu.VMEM((TILE, 2 * slots), jnp.bfloat16),
            pltpu.VMEM((5, 8, TILE), jnp.float32),
            pltpu.VMEM((5, 8, TILE), jnp.float32),
            pltpu.SemaphoreType.DMA((2 * STEPS, 2)),
            pltpu.SemaphoreType.DMA((2 * STEPS, 2)),
            pltpu.SemaphoreType.DMA((5,)),
            pltpu.SemaphoreType.DMA((5,)),
            pltpu.SemaphoreType.DMA((len(operands),)),
            pltpu.SemaphoreType.DMA((2,)),
        ],
        compiler_params=pltpu.CompilerParams(
            collective_id=0, has_side_effects=True, vmem_limit_bytes=VMEM_GRANT
        ),
    )(live_count.reshape(1, 2), *operands)
    out_high = out_high.reshape(125, 2, 4, TILE).transpose(2, 0, 1, 3).reshape(state_high.shape)
    return out_low, out_high, grad.reshape(-1)


def solution(mesh):
    placed = (
        P("groups", None, "domain"),
        P("groups", None, "domain"),
        P("groups", None, "domain"),
        P("groups", None, "domain"),
        P("domain"),
        P("domain"),
        P("domain"),
        P(None, "domain"),
        P(None, "domain"),
        P(None, "domain"),
        P("domain"),
        P("groups", "domain"),
        P("domain"),
    )
    return jax.shard_map(
        functools.partial(shards, mesh.shape["domain"]),
        mesh=mesh,
        in_specs=placed,
        out_specs=(
            P("groups", None, "domain"),
            P("groups", None, "domain"),
            P(("groups", "domain")),
        ),
        check_vma=False,
    )
```
